32 devices in a mesh: gx: 4 (over y, core), gy: 8 (over z, x).
Axes of the slice: x: 2, y: 2, z: 4, core: 2. Of those that a mesh axis runs over, the one named last changes fastest.
Arguments:
- adjoint_rhs: float32 [8, 8, 768, 128], P('gx', 'gy'), may hold values from -6 to 6
- local_inverse: bfloat16 [8, 8, 1024, 768], P('gx', 'gy')
- local_operator: bfloat16 [8, 8, 1024, 768], P('gx', 'gy')
- spill_rows: int32 [8, 8, 4, 64], P('gx', 'gy'), may hold values from 0 to 767, as said below
- coarse_basis: bfloat16 [8, 8, 64, 768], P('gx', 'gy'), may hold values from -3 to 3
- coarse_ids: int32 [8, 8, 64], P('gx', 'gy'), may hold values from 0 to 1023
- coarse_inverse: bfloat16 [1024, 1024], P(('gx', 'gy')), may hold values from -0.0008544922 to 0.0008544922
Outputs:
- adjoint_solution: float32 [8, 8, 768, 128], P('gx', 'gy')
- residual: float32 [8, 8, 768, 128], P('gx', 'gy')
The draws below stay inside these ranges and needn't reach their ends.
Inputs may be any that keep to these rules, and one draw needn't show every extreme that they name: Each list of spill_rows holds 64 distinct rows. `coarse_ids`: A coarse function may be listed more than once for a subdomain.
All inputs are finite; a program needn't handle non-finite values.
Results may differ from the reference program's by a relative error of at most 0.0041.
Values may be sent and summed in bfloat16 or wider, within the bound.
No kernel may reach another device: no remote copies, remote signals or barrier semaphores. Data moves between devices by JAX's collectives and lax.ppermute only.
A program may use at most 64 MiB of HBM per device.

```python
import math
import jax
import jax.numpy as jnp
from jax import lax

L = 1024
H = 64
OWN = 768
R = 128
KC = 64
NC = 1024
ITERS = 1
SUBX = 8
SUBY = 8


def near_identity(key, diagonal):
    noise_scale = 0.3 / math.sqrt(OWN)
    noise = jax.random.normal(key, (SUBX, SUBY, L, OWN), jnp.float32) * noise_scale
    return noise + diagonal * jnp.eye(L, OWN, dtype=jnp.float32)


def draw_local_inverse(key, part):
    return near_identity(jax.random.fold_in(key, 11), 0.5).astype(jnp.bfloat16)


def draw_local_operator(key, part):
    return near_identity(jax.random.fold_in(key, 23), 1.0).astype(jnp.bfloat16)


def pick_rows(one_key):
    return jax.random.permutation(one_key, OWN)[:H].astype(jnp.int32)


def draw_spill_rows(key, part):
    keys = jax.random.split(jax.random.fold_in(key, 37), SUBX * SUBY * 4)
    return jax.vmap(pick_rows)(keys).reshape(SUBX, SUBY, 4, H)


def touch_ends(values, own_key, low, top_value):
    longest = values.shape.index(max(values.shape))
    spots = []
    for shift in (0, 1):
        where = [jax.random.randint(jax.random.fold_in(own_key, axis), (), 0, length) for axis, length in enumerate(values.shape)]
        where[longest] = (where[longest] + shift) % values.shape[longest]
        spots.append(tuple(where))
    return values.at[spots[0]].set(low).at[spots[1]].set(top_value)


def levels(stream_key, dims, shards, smallest, largest):
    level = 1.0
    for axis_at, parts in shards:
        steps = jax.random.uniform(jax.random.fold_in(jax.random.fold_in(stream_key, 6), axis_at), (parts,), jnp.float32, smallest / len(shards), largest / len(shards))
        level = level * jnp.repeat(jnp.exp(steps), dims[axis_at] // parts).reshape((-1,) + (1,) * (len(dims) - 1 - axis_at))
    return level


def centred(stream_key, dims, scale, limit, cuts=(), kind=jnp.bfloat16):
    values = scale * jax.random.normal(stream_key, dims, jnp.float32)
    if cuts:
        values = values * levels(stream_key, dims, cuts, -0.22, 0.18)
    return jnp.clip(values, -limit, limit).astype(kind)


def setup_inputs(seed: int = 0) -> dict:
    key_of = jax.random.split(jax.random.key(seed), 8)
    return {
        "adjoint_rhs": centred(key_of[0], (SUBX, SUBY, OWN, R), 1.0, 6.0, ((0, 4), (1, 8)), jnp.float32),
        "local_inverse": draw_local_inverse(jax.random.fold_in(key_of[7], 71), 0),
        "local_operator": draw_local_operator(jax.random.fold_in(key_of[7], 71), 0),
        "spill_rows": draw_spill_rows(jax.random.fold_in(key_of[7], 71), 0),
        "coarse_basis": centred(key_of[4], (SUBX, SUBY, KC, OWN), 0.5, 3.0, ((0, 4), (1, 8))),
        "coarse_ids": touch_ends(jax.random.randint(key_of[5], (SUBX, SUBY, KC), 0, NC), jax.random.fold_in(key_of[5], 1), 0, NC - 1).astype(jnp.int32),
        "coarse_inverse": centred(key_of[6], (NC, NC), (KC * KC * OWN * SUBX * SUBY // 4) ** -0.5, 0.0008544922, ((0, 32),)),
    }


def from_lower(values, axis):
    zeros = jnp.zeros_like(lax.slice_in_dim(values, 0, 1, axis=axis))
    kept = lax.slice_in_dim(values, 0, values.shape[axis] - 1, axis=axis)
    return jnp.concatenate([zeros, kept], axis)


def from_upper(values, axis):
    zeros = jnp.zeros_like(lax.slice_in_dim(values, 0, 1, axis=axis))
    kept = lax.slice_in_dim(values, 1, values.shape[axis], axis=axis)
    return jnp.concatenate([kept, zeros], axis)


def add_rows(owned_rows, indices, values):
    return owned_rows.at[indices].add(values)


def spread(extended, spill_rows):
    owned_rows = extended[:, :, :OWN]
    groups = extended[:, :, OWN:].reshape(SUBX, SUBY, 4, H, R)
    from_west = from_lower(groups[:, :, 1], 0)
    from_east = from_upper(groups[:, :, 0], 0)
    from_south = from_lower(groups[:, :, 3], 1)
    from_north = from_upper(groups[:, :, 2], 1)
    received = jnp.stack([from_west, from_east, from_south, from_north], 2).reshape(SUBX * SUBY, 4 * H, R)
    indices = spill_rows.reshape(SUBX * SUBY, 4 * H)
    summed = jax.vmap(add_rows)(owned_rows.reshape(SUBX * SUBY, OWN, R), indices, received)
    return summed.reshape(SUBX, SUBY, OWN, R)


def block_product(pair):
    return jnp.dot(pair[0], pair[1], preferred_element_type=jnp.float32)


def apply_blocks(matrices, vectors):
    flat = lax.map(block_product, (matrices.reshape(SUBX * SUBY, L, OWN), vectors.astype(jnp.bfloat16).reshape(SUBX * SUBY, OWN, R)))
    return flat.reshape(SUBX, SUBY, L, R)


def reference(adjoint_rhs, local_inverse, local_operator, spill_rows, coarse_basis, coarse_ids, coarse_inverse):
    highest = lax.Precision.HIGHEST
    basis_rows = coarse_basis.astype(jnp.float32)
    residual = adjoint_rhs
    solution = jnp.zeros_like(adjoint_rhs)
    for iteration in range(ITERS):
        local_sol = apply_blocks(local_inverse, residual)
        terms = jnp.einsum('xykn,xynr->xykr', basis_rows, residual, precision=highest)
        coarse_rhs = jnp.zeros((NC, R), jnp.float32).at[coarse_ids.reshape(-1)].add(terms.reshape(-1, R))
        coarse_sol = jnp.dot(coarse_inverse.T, coarse_rhs.astype(jnp.bfloat16), preferred_element_type=jnp.float32)
        picked = coarse_sol[coarse_ids]
        coarse_part = jnp.einsum('xykn,xykr->xynr', basis_rows, picked, precision=highest)
        correction = spread(local_sol, spill_rows) + coarse_part
        solution = solution + correction
        image = apply_blocks(local_operator, correction)
        residual = residual - spread(image, spill_rows)
    return solution, residual
```

```python
import functools
import jax
import jax.numpy as jnp
from jax import lax
from jax.experimental import pallas as pl
from jax.experimental.pallas import tpu as pltpu
from jax.sharding import PartitionSpec as P

F32 = jnp.float32
BF16 = jnp.bfloat16
CONTRACT_FIRST = (((0,), (0,)), ((), ()))
VMEM = pl.BlockSpec(memory_space=pltpu.VMEM)
PARAMS = pltpu.CompilerParams(vmem_limit_bytes=24 * 1024 * 1024)


def bits_of(count):
    return count.bit_length() - 1


def mask_of(step):
    return (1 << step) - 1


def swap(value, axis, mask):
    count = lax.axis_size(axis)
    return lax.ppermute(value, axis, [(i, i ^ mask) for i in range(count)])


def relative_block(block, device, steps):
    left = block ^ device
    place = left * 0
    for step in range(steps, 0, -1):
        bit = (left >> (step - 1)) & 1
        place = place | (bit << (steps - step))
        left = left ^ (bit * mask_of(step))
    return place


def halves(value):
    high = value.astype(BF16)
    low = (value - high.astype(F32)).astype(BF16)
    return jnp.concatenate([high, low], axis=1)


def joined(value):
    width = value.shape[1] // 2
    return value[:, :width] + value[:, width:]


def mm(left, right):
    return jnp.dot(left, right, preferred_element_type=F32)


def terms_kernel(steps, rhs_ref, basis_ref, ids_ref, keep_ref, send_ref):
    device = lax.axis_index("gx")
    subs, _, functions, _ = basis_ref.shape
    half, width = keep_ref.shape
    order = 2 * half
    block = order >> steps
    total = None
    for s in range(subs):
        terms = joined(mm(basis_ref[s, 0], halves(rhs_ref[s, 0])))
        ids = ids_ref[s]
        place = relative_block(ids // block, device, steps) * block + ids % block
        rows = lax.broadcasted_iota(jnp.int32, (order, functions), 0)
        pick = (rows == place).astype(BF16)
        part = joined(mm(pick, halves(terms)))
        total = part if total is None else total + part
    keep_ref[...] = total[:half]
    send_ref[:half] = total[half:].astype(BF16)
    ids = jnp.concatenate([ids_ref[s] for s in range(subs)], axis=1)
    row = lax.broadcasted_iota(jnp.int32, (16, ids.shape[1]), 0)
    coded = jnp.where(row == 0, ids // 256, jnp.where(row == 1, ids % 256, 0))
    send_ref[half:] = coded.astype(F32).astype(BF16)


def halve_kernel(keep_ref, got_ref, own_ids_ref, next_ref, send_ref):
    rows = keep_ref.shape[0]
    half = rows // 2
    total = keep_ref[...] + got_ref[:rows].astype(F32)
    next_ref[...] = total[:half]
    send_ref[:half] = total[half:].astype(BF16)
    known = own_ids_ref.shape[0]
    send_ref[half : half + known] = own_ids_ref[...]
    send_ref[half + known :] = got_ref[rows:]


def sum_kernel(keep_ref, got_ref, halo_ref, next_ref, send_ref):
    rows = keep_ref.shape[0]
    total = keep_ref[...] + got_ref[:rows].astype(F32)
    next_ref[...] = total
    send_ref[:rows] = total.astype(BF16)
    send_ref[rows:] = halo_ref[...]


def solve_kernel(own_rows, inverse_ref, rhs_ref, own_ref, margin_ref):
    value = mm(inverse_ref[0, 0], rhs_ref[0, 0].astype(BF16))
    own_ref[0] = value[:own_rows]
    margin_ref[0] = value[own_rows:].astype(BF16)


def pick_kernel(masks, steps, near_ref, far_ref, *rest):
    id_refs, out_ref, scratch = rest[:-2], rest[-2], rest[-1]
    device = lax.axis_index("gy")
    half, order = near_ref.shape
    width = scratch.shape[1]
    rows = 2 * half
    per_device = rows >> steps
    place = lax.broadcasted_iota(jnp.int32, (rows, rows), 1)
    target = lax.broadcasted_iota(jnp.int32, (rows, rows), 0)
    piece = place // per_device
    source = piece * 0 + device
    for bit, mask in enumerate(masks):
        source = source ^ (((piece >> bit) & 1) * mask)
    arrange = (source * per_device + place % per_device == target).astype(BF16)
    names = lax.broadcasted_iota(jnp.int32, (order, width), 0)
    near = near_ref[...]
    far = far_ref[...]
    for q, ref in enumerate(id_refs):
        code = ref[...].astype(F32)
        ids = (code[0:1] * 256.0 + code[1:2]).astype(jnp.int32)
        pick = (names == ids).astype(BF16)
        scratch[:half] = mm(near, pick).astype(BF16)
        scratch[half:] = mm(far, pick).astype(BF16)
        value = mm(arrange, scratch[...])
        out_ref[q * width : (q + 1) * width] = value.T.astype(BF16)


def coarse_kernel(rows, picked_ref, keep_ref, halo_ref, *rest):
    got_refs, next_ref, send_ref = rest[:-2], rest[-2], rest[-1]
    total = keep_ref[...]
    for ref in got_refs:
        total = total + ref[:rows].astype(F32)
    low = total.astype(BF16)
    half = next_ref.shape[0]
    value = mm(picked_ref[...], low)
    next_ref[...] = value[:half]
    send_ref[:half] = value[half:].astype(BF16)
    send_ref[half:] = halo_ref[...]


def halve_halo_kernel(keep_ref, got_ref, halo_ref, next_ref, send_ref):
    rows = keep_ref.shape[0]
    half = rows // 2
    total = keep_ref[...] + got_ref[:rows].astype(F32)
    next_ref[...] = total[:half]
    send_ref[:half] = total[half:].astype(BF16)
    send_ref[half:] = halo_ref[...]


def spread_pick(rows, spill):
    iota = lax.broadcasted_iota(jnp.int32, (rows, spill.shape[1]), 0)
    return (iota == spill).astype(BF16)


def received(subs, sub, width, groups, pair_x, other_x, pair_y, other_y, even_x, even_y):
    west = groups(sub - 1, 1) if sub > 0 else jnp.where(even_x, other_x, pair_x)
    east = groups(sub + 1, 0) if sub < subs - 1 else jnp.where(even_x, pair_x, other_x)
    rows = slice(sub * width, (sub + 1) * width)
    south = jnp.where(even_y, other_y[rows], pair_y[rows])
    north = jnp.where(even_y, pair_y[rows], other_y[rows])
    return jnp.concatenate([west, east, south, north], axis=0)


def other_neighbour(axis):
    device = lax.axis_index(axis)
    even = device % 2 == 0
    other = jnp.where(even, device - 1, device + 1)
    return device, even, other


def correction_kernel(
    counts, width, own_ref, margin_ref, spill_ref, basis_ref, operator_ref, keep_ref, *rest
):
    gx_first, gx_later, gy_first, gy_later = counts
    refs = list(rest)
    pair_x_ref = refs.pop(0)
    last_refs = [refs.pop(0) for _ in range(gx_later)]
    pair_y_ref = refs.pop(0)
    later_y = [refs.pop(0) for _ in range(gy_later)]
    out_ref, low_ref, image_ref, send_xp, send_xo, send_yp, send_yo = refs
    subs, rows, columns = own_ref.shape
    functions = basis_ref.shape[2]
    picked = keep_ref[...]
    count = picked.shape[0]
    final_ref = last_refs[-1] if last_refs else pair_x_ref
    picked = picked + final_ref[:count].astype(F32)
    _, even_x, _ = other_neighbour("gx")
    _, even_y, _ = other_neighbour("gy")
    top = pair_x_ref.shape[0] - width
    pair_x = pair_x_ref[top:]
    other_x = None
    device_x, _, other_dev = other_neighbour("gx")
    for step, ref in enumerate(last_refs, 2):
        here = (device_x ^ mask_of(step)) == other_dev
        part = jnp.where(here, ref[ref.shape[0] - width :], jnp.zeros((width, columns), BF16))
        other_x = part if other_x is None else other_x + part
    if other_x is None:
        other_x = jnp.zeros((width, columns), BF16)
    size = subs * width
    pair_y = pair_y_ref[pair_y_ref.shape[0] - size :]
    other_y = jnp.zeros((size, columns), BF16)
    device_y, _, other_dev = other_neighbour("gy")
    for step, ref in enumerate(later_y, 2):
        here = (device_y ^ mask_of(step)) == other_dev
        other_y = other_y + jnp.where(
            here, ref[ref.shape[0] - size :], jnp.zeros((size, columns), BF16)
        )

    def groups(sub, side):
        return margin_ref[sub, side * width : (side + 1) * width]

    for s in range(subs):
        values = received(
            subs, s, width, groups, pair_x, other_x, pair_y, other_y, even_x, even_y
        )
        coarse = lax.dot_general(
            basis_ref[s, 0],
            halves(picked[s * functions : (s + 1) * functions]),
            CONTRACT_FIRST,
            preferred_element_type=F32,
        )
        value = own_ref[s] + mm(spread_pick(rows, spill_ref[s]), values) + joined(coarse)
        out_ref[s, 0] = value
        low = value.astype(BF16)
        low_ref[s] = low
        image_ref[s] = mm(operator_ref[s, 0], low).astype(BF16)

    def side(sub, number):
        return image_ref[sub, number * width : (number + 1) * width]

    west, east = side(0, 0), side(subs - 1, 1)
    send_xp[...] = jnp.where(even_x, east, west)
    send_xo[...] = jnp.where(even_x, west, east)
    for s in range(subs):
        south, north = side(s, 2), side(s, 3)
        send_yp[s * width : (s + 1) * width] = jnp.where(even_y, north, south)
        send_yo[s * width : (s + 1) * width] = jnp.where(even_y, south, north)


def image_kernel(operator_ref, low_ref, rhs_ref, out_ref):
    for s in range(low_ref.shape[0]):
        out_ref[s] = rhs_ref[s, 0] - mm(operator_ref[s, 0], low_ref[s])


def residual_kernel(
    width, part_ref, image_ref, spill_ref, xp_ref, xo_ref, yp_ref, yo_ref, out_ref
):
    subs, rows, _ = part_ref.shape
    _, even_x, _ = other_neighbour("gx")
    _, even_y, _ = other_neighbour("gy")

    def groups(sub, side):
        return image_ref[sub, side * width : (side + 1) * width]

    for s in range(subs):
        values = received(
            subs, s, width, groups, xp_ref[...], xo_ref[...], yp_ref[...], yo_ref[...],
            even_x, even_y,
        )
        out_ref[s, 0] = part_ref[s] - mm(spread_pick(rows, spill_ref[s]), values)


def call(kernel, shapes, *args, scratch=(), name=None):
    return pl.pallas_call(
        kernel,
        out_shape=[jax.ShapeDtypeStruct(shape, dtype) for shape, dtype in shapes],
        in_specs=[VMEM] * len(args),
        out_specs=[VMEM] * len(shapes),
        scratch_shapes=list(scratch),
        compiler_params=PARAMS,
        name=name,
    )(*args)


def body(
    adjoint_rhs, local_inverse, local_operator, spill_rows, coarse_basis, coarse_ids, coarse_inverse
):
    subs, _, rows, width = adjoint_rhs.shape
    extended = local_inverse.shape[2]
    margin = spill_rows.shape[3]
    functions = coarse_ids.shape[2]
    order = coarse_inverse.shape[1]
    count_x, count_y = lax.axis_size("gx"), lax.axis_size("gy")
    steps_x, steps_y = bits_of(count_x), bits_of(count_y)
    listed = subs * functions
    spill = spill_rows.reshape(subs, 1, 4 * margin)

    keep, send = call(
        functools.partial(terms_kernel, steps_x),
        [((order // 2, width), F32), ((order // 2 + 16, listed), BF16)],
        adjoint_rhs, coarse_basis, coarse_ids, name="coarse_terms",
    )
    ids_known = [send[order // 2 :]]
    got = swap(send, "gx", mask_of(1))

    own, margins = pl.pallas_call(
        functools.partial(solve_kernel, rows),
        grid=(subs,),
        out_shape=[
            jax.ShapeDtypeStruct((subs, rows, width), F32),
            jax.ShapeDtypeStruct((subs, 4 * margin, width), BF16),
        ],
        in_specs=[
            pl.BlockSpec((1, 1, extended, rows), lambda s: (s, 0, 0, 0)),
            pl.BlockSpec((1, 1, rows, width), lambda s: (s, 0, 0, 0)),
        ],
        out_specs=[
            pl.BlockSpec((1, rows, width), lambda s: (s, 0, 0)),
            pl.BlockSpec((1, 4 * margin, width), lambda s: (s, 0, 0)),
        ],
        compiler_params=PARAMS,
        name="local_solve",
    )(local_inverse, adjoint_rhs)

    even_x = lax.axis_index("gx") % 2 == 0
    even_y = lax.axis_index("gy") % 2 == 0
    groups = margins.reshape(subs, 4, margin, width)
    west, east = groups[0, 0], groups[subs - 1, 1]
    south = groups[:, 2].reshape(subs * margin, width)
    north = groups[:, 3].reshape(subs * margin, width)
    halo_xp, halo_xo = jnp.where(even_x, east, west), jnp.where(even_x, west, east)
    halo_yp, halo_yo = jnp.where(even_y, north, south), jnp.where(even_y, south, north)

    size = order // 2
    for step in range(2, steps_x + 1):
        own_ids = jnp.concatenate(ids_known, 0)
        known = own_ids.shape[0]
        half = size // 2
        keep, send = call(
            halve_kernel,
            [((half, width), F32), ((half + 2 * known, listed), BF16)],
            keep, got, own_ids, name="coarse_halve",
        )
        ids_known = ids_known + [
            got[size + 16 * i : size + 16 * (i + 1)] for i in range(len(ids_known))
        ]
        got = swap(send, "gx", mask_of(step))
        size = half
    ids_known = ids_known + [
        got[size + 16 * i : size + 16 * (i + 1)] for i in range(len(ids_known))
    ]
    ordered = []
    for q in range(count_x):
        p = sum(((q >> (steps_x - k)) & 1) << (k - 1) for k in range(1, steps_x + 1))
        ordered.append(ids_known[p])

    gather_masks = [1 << (steps_y - 1 - i) for i in range(steps_y)]
    near, far = coarse_inverse, None
    for i, mask in enumerate(gather_masks):
        far = swap(near, "gy", mask)
        if i < steps_y - 1:
            near = jnp.concatenate([near, far], 0)
    (picked,) = call(
        functools.partial(pick_kernel, gather_masks, steps_y),
        [((count_x * listed, size), BF16)],
        near, far, *ordered,
        scratch=[pltpu.VMEM((size, listed), BF16)],
        name="inverse_pick",
    )

    halo_rows = subs * margin
    keep, send = call(
        sum_kernel,
        [((size, width), F32), ((size + halo_rows, width), BF16)],
        keep, got, halo_yp, name="coarse_sum_x",
    )
    got = swap(send, "gy", mask_of(1))
    pair_y = got
    later_y = []
    pending = [got]
    step = 2
    while step <= steps_y:
        keep, send = call(
            sum_kernel,
            [((size, width), F32), ((size + halo_rows, width), BF16)],
            keep, pending[0], halo_yo, name="coarse_sum_y",
        )
        if step < steps_y:
            first = swap(send, "gy", mask_of(step))
            second = swap(send, "gy", mask_of(step + 1))
            third = swap(send[:size], "gy", mask_of(step) ^ mask_of(step + 1))
            later_y += [first, second]
            pending = [first, second, third]
            step += 2
        else:
            first = swap(send, "gy", mask_of(step))
            later_y += [first]
            pending = [first]
            step += 1
        if step <= steps_y:
            while len(pending) > 1:
                extra = pending.pop()
                keep = keep + extra[:size].astype(F32)

    half = count_x * listed // 2
    keep, send = call(
        functools.partial(coarse_kernel, size),
        [((half, width), F32), ((half + margin, width), BF16)],
        picked, keep, halo_xp, *pending, name="coarse_solve",
    )
    pair_x = swap(send, "gx", mask_of(1))
    got = pair_x
    later_x = []
    for step in range(2, steps_x + 1):
        half = half // 2
        keep, send = call(
            halve_halo_kernel,
            [((half, width), F32), ((half + margin, width), BF16)],
            keep, got, halo_xo, name="picked_halve",
        )
        got = swap(send, "gx", mask_of(step))
        later_x.append(got)

    full = lambda shape: pl.BlockSpec(shape, lambda i: (0,) * len(shape))
    inputs = [own, margins, spill, coarse_basis, local_operator, keep, pair_x, *later_x, pair_y, *later_y]
    in_specs = [full(x.shape) for x in inputs]
    in_specs[4] = pl.BlockSpec(
        (subs, 1, extended - rows, rows), lambda i: (0, 0, rows // (extended - rows), 0)
    )
    shapes = [
        ((subs, 1, rows, width), F32),
        ((subs, rows, width), BF16),
        ((subs, 4 * margin, width), BF16),
        ((margin, width), BF16),
        ((margin, width), BF16),
        ((subs * margin, width), BF16),
        ((subs * margin, width), BF16),
    ]
    correction, low, image, send_xp, send_xo, send_yp, send_yo = pl.pallas_call(
        functools.partial(correction_kernel, (1, len(later_x), 1, len(later_y)), margin),
        grid=(1,),
        out_shape=[jax.ShapeDtypeStruct(*s) for s in shapes],
        in_specs=in_specs,
        out_specs=[full(s[0]) for s in shapes],
        compiler_params=PARAMS,
        name="correction",
    )(*inputs)

    def other(value, axis):
        count = lax.axis_size(axis)
        pairs = [(i, i + 1) for i in range(1, count - 1, 2)]
        return lax.ppermute(value, axis, pairs + [(j, i) for i, j in pairs])

    got_xo = other(send_xo, "gx")
    got_yp = swap(send_yp, "gy", 1)
    got_yo = other(send_yo, "gy")
    got_xp = swap(send_xp, "gx", 1)

    (part,) = pl.pallas_call(
        image_kernel,
        grid=(1,),
        out_shape=[jax.ShapeDtypeStruct((subs, rows, width), F32)],
        in_specs=[
            full((subs, 1, rows, rows)),
            full((subs, rows, width)),
            full((subs, 1, rows, width)),
        ],
        out_specs=[full((subs, rows, width))],
        compiler_params=PARAMS,
        name="image_own",
    )(local_operator, low, adjoint_rhs)
    (residual,) = call(
        functools.partial(residual_kernel, margin),
        [((subs, 1, rows, width), F32)],
        part, image, spill, got_xp, got_xo, got_yp, got_yo, name="residual",
    )
    return correction, residual


def solution(mesh):
    in_specs = (
        P("gx", "gy", None, None),
        P("gx", "gy", None, None),
        P("gx", "gy", None, None),
        P("gx", "gy", None, None),
        P("gx", "gy", None, None),
        P("gx", "gy", None),
        P(("gx", "gy"), None),
    )
    out_specs = (P("gx", "gy", None, None), P("gx", "gy", None, None))
    return jax.shard_map(body, mesh=mesh, in_specs=in_specs, out_specs=out_specs, check_vma=False)
```

```python
import functools
import jax
import jax.numpy as jnp
from jax import lax
from jax.experimental import pallas as pl
from jax.experimental.pallas import tpu as pltpu
from jax.sharding import PartitionSpec as P

F32 = jnp.float32
BF16 = jnp.bfloat16
CONTRACT_FIRST = (((0,), (0,)), ((), ()))


def bits_of(count):
    return count.bit_length() - 1


def mask_of(step):
    return (1 << step) - 1


def mirror(bit):
    return (2 << bit) - 2


def swap(value, axis, mask):
    count = lax.axis_size(axis)
    return lax.ppermute(value, axis, [(i, i ^ mask) for i in range(count)])


def other(value, axis, closed=False):
    count = lax.axis_size(axis)
    pairs = [(i, i + 1) for i in range(1, count - 1, 2)] + [(0, count - 1)] * closed
    return lax.ppermute(value, axis, pairs + [(j, i) for i, j in pairs])


def relative_block(block, device, steps):
    left = block ^ device
    place = left * 0
    for step in range(steps, 0, -1):
        bit = (left >> (step - 1)) & 1
        place = place | (bit << (steps - step))
        left = left ^ (bit * mask_of(step))
    return place


def halves(value):
    high = value.astype(BF16)
    low = (value - high.astype(F32)).astype(BF16)
    return jnp.concatenate([high, low], axis=1)


def joined(value):
    width = value.shape[1] // 2
    return value[:, :width] + value[:, width:]


def mm(left, right):
    return jnp.dot(left, right, preferred_element_type=F32)


def copies_of(pairs, semaphores):
    copies = [
        pltpu.make_async_copy(source, target, semaphores.at[i])
        for i, (source, target) in enumerate(pairs)
    ]
    for copy in copies:
        copy.start()
    return copies


def terms_kernel(
    steps, rhs_hbm, basis_hbm, ids_hbm, keep_ref, send_ref, low_ref, rhs_ref, basis_ref, ids_ref, sems
):
    device = lax.axis_index("gx")
    subs, functions, _ = basis_ref.shape
    pairs = [(ids_hbm, ids_ref)]
    for s in range(subs):
        pairs += [(basis_hbm.at[s, 0], basis_ref.at[s]), (rhs_hbm.at[s, 0], rhs_ref.at[s])]
    copies = copies_of(pairs, sems)
    half, width = keep_ref.shape
    order = 2 * half
    block = order >> steps
    copies[0].wait()
    ids = jnp.concatenate([ids_ref[s] for s in range(subs)], axis=1)
    row = lax.broadcasted_iota(jnp.int32, (16, ids.shape[1]), 0)
    coded = jnp.where(row == 0, ids // 256, jnp.where(row == 1, ids % 256, 0))
    send_ref[half:] = coded.astype(F32).astype(BF16)
    place = relative_block(ids // block, device, steps) * block + ids % block
    rows = lax.broadcasted_iota(jnp.int32, (order, ids.shape[1]), 0)
    pick = (rows == place).astype(BF16)
    terms = []
    for s in range(subs):
        copies[1 + 2 * s].wait()
        copies[2 + 2 * s].wait()
        value = rhs_ref[s]
        high = value.astype(BF16)
        low = (value - high.astype(F32)).astype(BF16)
        low_ref[s] = high
        terms.append(joined(mm(basis_ref[s], jnp.concatenate([high, low], axis=1))))
    total = joined(mm(pick, halves(jnp.concatenate(terms, axis=0))))
    keep_ref[...] = total[:half]
    send_ref[:half] = total[half:].astype(BF16)


def halve_kernel(known, keep_ref, got_ref, sent_ref, next_ref, send_ref):
    rows = keep_ref.shape[0]
    half = rows // 2
    total = keep_ref[...] + got_ref[:rows].astype(F32)
    next_ref[...] = total[:half]
    send_ref[:half] = total[half:].astype(BF16)
    send_ref[half : half + known] = sent_ref[rows:]
    send_ref[half + known :] = got_ref[rows:]


def join_kernel(near_ref, far_ref, token_ref, out_ref):
    rows = near_ref.shape[0]
    out_ref[:rows] = near_ref[...]
    out_ref[rows:] = far_ref[...]


def sum_kernel(keep_ref, got_ref, *rest):
    halo_refs, next_ref, send_ref = rest[:-2], rest[-2], rest[-1]
    rows = keep_ref.shape[0]
    total = keep_ref[...] + got_ref[:rows].astype(F32)
    next_ref[...] = total
    send_ref[:rows] = total.astype(BF16)
    at = rows
    for ref in halo_refs:
        send_ref[at : at + ref.shape[0]] = ref[...]
        at += ref.shape[0]


def forward_kernel(keep_ref, got_ref, next_ref, send_ref):
    rows = keep_ref.shape[0]
    total = keep_ref[...] + got_ref[:rows].astype(F32)
    next_ref[...] = total
    send_ref[:rows] = total.astype(BF16)
    start = got_ref.shape[0] - (send_ref.shape[0] - rows)
    send_ref[rows:] = got_ref[start:]


def outward(width, groups, subs, send_xp, send_xo, send_yp, send_yo):
    even_x = lax.axis_index("gx") % 2 == 0
    even_y = lax.axis_index("gy") % 2 == 0
    west, east = groups(0, 0), groups(subs - 1, 1)
    send_xp[...] = jnp.where(even_x, east, west)
    send_xo[...] = jnp.where(even_x, west, east)
    for s in range(subs):
        south, north = groups(s, 2), groups(s, 3)
        send_yp[s * width : (s + 1) * width] = jnp.where(even_y, north, south)
        send_yo[s * width : (s + 1) * width] = jnp.where(even_y, south, north)


def solve_kernel(width, inverse_ref, rhs_ref, token_ref, own_ref, margin_ref, *sends):
    subs, rows, _ = own_ref.shape
    for s in range(subs):
        value = mm(inverse_ref[s, 0], rhs_ref[s])
        own_ref[s] = value[:rows]
        margin_ref[s] = value[rows:].astype(BF16)

    def groups(sub, number):
        return margin_ref[sub, number * width : (number + 1) * width]

    outward(width, groups, subs, *sends)


def pick_kernel(places, rows_ref, token_ref, *rest):
    id_refs, out_ref = rest[:-1], rest[-1]
    order = rows_ref.shape[1]
    width = id_refs[0].shape[1]
    names = lax.broadcasted_iota(jnp.int32, (order, width), 0)
    rows = rows_ref[...]
    for q, (holder, start) in enumerate(places):
        code = id_refs[holder][start : start + 16].astype(F32)
        ids = (code[0:1] * 256.0 + code[1:2]).astype(jnp.int32)
        pick = (names == ids).astype(BF16)
        out_ref[q * width : (q + 1) * width] = mm(rows, pick).T.astype(BF16)


def arranged(low, masks, first):
    device = lax.axis_index("gy")
    rows = low.shape[0]
    per_device = rows >> len(masks)
    half = rows // 2
    place = lax.broadcasted_iota(jnp.int32, (half, rows), 0) + first
    target = lax.broadcasted_iota(jnp.int32, (half, rows), 1)
    piece = place // per_device
    source = piece * 0 + device
    for bit, mask in enumerate(masks):
        source = source ^ (((piece >> bit) & 1) * mask)
    pick = (source * per_device + place % per_device == target).astype(BF16)
    return mm(pick, low).astype(BF16)


def coarse_kernel(rows, masks, near_ref, far_ref, keep_ref, halo_ref, *rest):
    got_refs, next_ref, send_ref = rest[:-2], rest[-2], rest[-1]
    total = keep_ref[...]
    for ref in got_refs:
        total = total + ref[:rows].astype(F32)
    low = total.astype(BF16)
    half = next_ref.shape[0]
    value = mm(near_ref[...], arranged(low, masks, 0))
    value = value + mm(far_ref[...], arranged(low, masks, rows // 2))
    next_ref[...] = value[:half]
    send_ref[:half] = value[half:].astype(BF16)
    send_ref[half:] = halo_ref[...]


def halve_halo_kernel(keep_ref, got_ref, halo_ref, next_ref, send_ref):
    rows = keep_ref.shape[0]
    half = rows // 2
    total = keep_ref[...] + got_ref[:rows].astype(F32)
    next_ref[...] = total[:half]
    send_ref[:half] = total[half:].astype(BF16)
    send_ref[half:] = halo_ref[...]


def spread_pick(rows, spill):
    spill = jnp.concatenate([spill[d : d + 1] for d in range(4)], axis=1)
    iota = lax.broadcasted_iota(jnp.int32, (rows, spill.shape[1]), 0)
    return (iota == spill).astype(BF16)


def received(subs, sub, width, groups, pair_x, other_x, pair_y, other_y, even_x, even_y):
    west = groups(sub - 1, 1) if sub > 0 else jnp.where(even_x, other_x, pair_x)
    east = groups(sub + 1, 0) if sub < subs - 1 else jnp.where(even_x, pair_x, other_x)
    rows = slice(sub * width, (sub + 1) * width)
    south = jnp.where(even_y, other_y[rows], pair_y[rows])
    north = jnp.where(even_y, pair_y[rows], other_y[rows])
    return jnp.concatenate([west, east, south, north], axis=0)


def other_neighbour(axis):
    device = lax.axis_index(axis)
    even = device % 2 == 0
    other = jnp.where(even, device - 1, device + 1)
    return device, even, other


def from_other(axis, refs, masks, distance):
    device, even, _ = other_neighbour(axis)
    source = jnp.where(even, device - distance, device + distance)
    size, refs = refs
    value = jnp.zeros((size, refs[0].shape[1]), BF16)
    for ref, mask in zip(refs, masks):
        value = jnp.where((device ^ mask) == source, ref[ref.shape[0] - size :], value)
    return even, value


def correction_kernel(
    count_x, width, own_ref, margin_ref, spill_ref, basis_ref, operator_ref, keep_ref, *rest
):
    x_refs, rest = rest[:count_x], rest[count_x:]
    y_refs, (out_ref, low_ref, image_ref, *sends) = rest[:-7], rest[-7:]
    subs, rows, columns = own_ref.shape
    functions = basis_ref.shape[2]
    picked = keep_ref[...] + x_refs[-1][: keep_ref.shape[0]].astype(F32)
    halo = subs * width
    x_masks = [mask_of(step) for step in range(2, len(x_refs) + 1)]
    y_masks = [mirror(bit) for bit in range(1, len(y_refs))]
    even_x, other_x = from_other("gx", (width, x_refs[1:]), x_masks, 1)
    even_y, other_y = from_other("gy", (halo, y_refs[1:]), y_masks, 2)
    pair_x = x_refs[0][x_refs[0].shape[0] - width :]
    first = y_refs[0].shape[0] - 2 * halo
    pair_y = y_refs[0][first : first + halo]

    def margins(sub, number):
        return margin_ref[sub, number * width : (number + 1) * width]

    for s in range(subs):
        values = received(
            subs, s, width, margins, pair_x, other_x, pair_y, other_y, even_x, even_y
        )
        part = picked[s * functions : (s + 1) * functions]
        high = part.astype(BF16)
        low = (part - high.astype(F32)).astype(BF16)
        basis = basis_ref[s, 0]
        coarse = lax.dot_general(
            jnp.concatenate([basis, basis], axis=0),
            jnp.concatenate([high, low], axis=0),
            CONTRACT_FIRST,
            preferred_element_type=F32,
        )
        value = own_ref[s] + mm(spread_pick(rows, spill_ref[s, 0]), values) + coarse
        out_ref[s] = value
        low = value.astype(BF16)
        low_ref[s] = low
        image_ref[s] = mm(operator_ref[s, 0, rows:], low).astype(BF16)

    def images(sub, number):
        return image_ref[sub, number * width : (number + 1) * width]

    outward(width, images, subs, *sends)


def image_kernel(operator_ref, low_ref, rhs_ref, correction_ref, part_ref, out_ref, sems):
    subs, rows, _ = low_ref.shape
    copies = copies_of([(correction_ref.at[s], out_ref.at[s, 0]) for s in range(subs)], sems)
    for s in range(subs):
        part_ref[s] = rhs_ref[s, 0] - mm(operator_ref[s, 0, :rows], low_ref[s])
    for copy in copies:
        copy.wait()


def residual_kernel(
    width, part_ref, image_ref, spill_ref, xp_ref, xo_ref, yp_ref, yo_ref, out_ref, value_ref, sems
):
    subs, rows, _ = part_ref.shape
    even_x = lax.axis_index("gx") % 2 == 0
    even_y = lax.axis_index("gy") % 2 == 0

    def margins(sub, number):
        return image_ref[sub, number * width : (number + 1) * width]

    device, count = lax.axis_index("gx"), lax.axis_size("gx")
    inner = jnp.logical_and(device != 0, device != count - 1)
    other_x = jnp.where(inner, xo_ref[...], jnp.zeros(xo_ref.shape, BF16))
    copies = []
    for s in range(subs):
        values = received(
            subs, s, width, margins, xp_ref[...], other_x, yp_ref[...], yo_ref[...],
            even_x, even_y,
        )
        value_ref[s] = part_ref[s] - mm(spread_pick(rows, spill_ref[s, 0]), values)
        copies.append(pltpu.make_async_copy(value_ref.at[s], out_ref.at[s, 0], sems.at[s]))
        copies[s].start()
    for copy in copies:
        copy.wait()


VMEM = pl.BlockSpec(memory_space=pltpu.VMEM)
HBM = pl.BlockSpec(memory_space=pltpu.HBM)
ANY = pl.BlockSpec(memory_space=pl.ANY)
MIB = 1024 * 1024


def call(kernel, outs, args, name, scratch=(), ins=None, out_specs=None, limit=4, cost=10**9):
    return pl.pallas_call(
        kernel,
        out_shape=[jax.ShapeDtypeStruct(shape, dtype) for shape, dtype in outs],
        in_specs=ins or [VMEM] * len(args),
        out_specs=out_specs or [VMEM] * len(outs),
        scratch_shapes=list(scratch),
        compiler_params=pltpu.CompilerParams(vmem_limit_bytes=limit * MIB),
        cost_estimate=pl.CostEstimate(flops=cost, bytes_accessed=MIB, transcendentals=0),
        name=name,
    )(*args)


def body(
    adjoint_rhs, local_inverse, local_operator, spill_rows, coarse_basis, coarse_ids, coarse_inverse
):
    subs, _, rows, width = adjoint_rhs.shape
    margin = spill_rows.shape[3]
    functions = coarse_ids.shape[2]
    order = coarse_inverse.shape[1]
    count_x, count_y = lax.axis_size("gx"), lax.axis_size("gy")
    steps_x, steps_y = bits_of(count_x), bits_of(count_y)
    listed = subs * functions
    halo = subs * margin
    dma = pltpu.SemaphoreType.DMA
    block = (subs, rows, width)
    messages = [((margin, width), BF16)] * 2 + [((halo, width), BF16)] * 2

    gather_masks = [1 << (steps_y - 1 - i) for i in range(steps_y)]
    near = coarse_inverse
    far = swap(near, "gy", gather_masks[0])

    size = order // 2
    keep, send, low = call(
        functools.partial(terms_kernel, steps_x),
        [((size, width), F32), ((size + 16, listed), BF16), (block, BF16)],
        [pltpu.with_memory_space_constraint(x, pltpu.HBM) for x in (adjoint_rhs, coarse_basis, coarse_ids)],
        "coarse_terms",
        ins=[HBM] * 3,
        scratch=[
            pltpu.VMEM(block, F32),
            pltpu.VMEM((subs, functions, rows), BF16),
            pltpu.VMEM(coarse_ids.shape, jnp.int32),
            dma((1 + 2 * subs,)),
        ],
        limit=12,
    )
    got = swap(send, "gx", mask_of(1))
    id_places = [(send, size, 0)]
    for step in range(2, steps_x + 1):
        half = size // 2
        known = 16 * len(id_places)
        id_places = id_places + [(got, size + 16 * i, 0) for i in range(len(id_places))]
        keep, send = call(
            functools.partial(halve_kernel, known),
            [((half, width), F32), ((half + 2 * known, listed), BF16)],
            [keep, got, send],
            "coarse_halve",
        )
        got = swap(send, "gx", mask_of(step))
        size = half
    id_places = id_places + [(got, size + 16 * i, 0) for i in range(len(id_places))]

    own, margins, halo_xp, halo_xo, halo_yp, halo_yo = call(
        functools.partial(solve_kernel, margin),
        [(block, F32), ((subs, 4 * margin, width), BF16)] + messages,
        [local_inverse, low, send],
        "local_solve",
        ins=[VMEM, VMEM, ANY],
        limit=12,
    )

    def join(near, far, token):
        shape = (2 * near.shape[0], near.shape[1])
        return call(
            join_kernel, [(shape, BF16)], [near, far, token], "inverse_join", ins=[VMEM, VMEM, ANY]
        )[0]

    near = join(near, far, own)
    far = swap(near, "gy", gather_masks[1])

    keep, send = call(
        sum_kernel,
        [((size, width), F32), ((size + 2 * halo, width), BF16)],
        [keep, got, halo_yp, halo_yo],
        "coarse_sum",
    )
    got = swap(send, "gy", mask_of(1))
    y_got = [got]
    for mask in gather_masks[2:]:
        near = join(near, far, got)
        far = swap(near, "gy", mask)
    pending = [got]
    bit = 1
    while bit < steps_y:
        for extra in pending[1:]:
            keep = keep + extra[:size].astype(F32)
        keep, send = call(
            forward_kernel,
            [((size, width), F32), ((size + halo, width), BF16)],
            [keep, pending[0]],
            "coarse_sum",
        )
        masks = [mirror(bit)] + [mirror(bit + 1)] * (bit + 1 < steps_y)
        pending = [swap(send, "gy", mask) for mask in masks]
        y_got += pending
        if len(masks) > 1:
            pending.append(swap(send[:size], "gy", masks[0] ^ masks[1]))
        bit += 2

    holders, places = [], []
    for q in range(count_x):
        p = sum(((q >> (steps_x - k)) & 1) << (k - 1) for k in range(1, steps_x + 1))
        array, start, _ = id_places[p]
        found = [i for i, holder in enumerate(holders) if holder is array]
        if not found:
            holders.append(array)
            found = [len(holders) - 1]
        places.append((found[0], start))
    def picked(value, token):
        return call(
            functools.partial(pick_kernel, places),
            [((count_x * listed, value.shape[0]), BF16)],
            [value, token, *holders],
            "inverse_pick",
            ins=[VMEM, ANY] + [VMEM] * len(holders),
            limit=8,
        )[0]

    near, far = picked(near, send), picked(far, send)

    half = count_x * listed // 2
    keep, send = call(
        functools.partial(coarse_kernel, size, gather_masks),
        [((half, width), F32), ((half + margin, width), BF16)],
        [near, far, keep, halo_xp, *pending],
        "coarse_solve",
    )
    x_got = [swap(send, "gx", mask_of(1))]
    for step in range(2, steps_x + 1):
        half = half // 2
        keep, send = call(
            halve_halo_kernel,
            [((half, width), F32), ((half + margin, width), BF16)],
            [keep, x_got[-1], halo_xo],
            "picked_halve",
        )
        x_got.append(swap(send, "gx", mask_of(step)))

    correction, low, image, *sends = call(
        functools.partial(correction_kernel, len(x_got), margin),
        [(block, F32), (block, BF16), ((subs, 4 * margin, width), BF16)] + messages,
        [own, margins, spill_rows, coarse_basis, local_operator, keep, *x_got, *y_got],
        "correction",
        limit=12,
    )

    got_yo = other(sends[3], "gy")
    got_xo = other(sends[1], "gx", closed=True)
    got_yp = swap(sends[2], "gy", 1)
    got_xp = swap(sends[0], "gx", 1)

    part, correction = call(
        image_kernel,
        [(block, F32), (adjoint_rhs.shape, F32)],
        [local_operator, low, adjoint_rhs, correction],
        "image_own",
        out_specs=[VMEM, HBM],
        scratch=[dma((subs,))],
        limit=12,
    )
    (residual,) = call(
        functools.partial(residual_kernel, margin),
        [(adjoint_rhs.shape, F32)],
        [part, image, spill_rows, got_xp, got_xo, got_yp, got_yo],
        "residual",
        out_specs=[HBM],
        scratch=[pltpu.VMEM(block, F32), dma((subs,))],
    )
    return correction, residual


def solution(mesh):
    in_specs = (
        P("gx", "gy", None, None),
        P("gx", "gy", None, None),
        P("gx", "gy", None, None),
        P("gx", "gy", None, None),
        P("gx", "gy", None, None),
        P("gx", "gy", None),
        P(("gx", "gy"), None),
    )
    out_specs = (P("gx", "gy", None, None), P("gx", "gy", None, None))
    return jax.shard_map(body, mesh=mesh, in_specs=in_specs, out_specs=out_specs, check_vma=False)
```

```python
import functools
import jax
import jax.numpy as jnp
from jax import lax
from jax.experimental import pallas as pl
from jax.experimental.pallas import tpu as pltpu
from jax.sharding import PartitionSpec as P

F32 = jnp.float32
BF16 = jnp.bfloat16
CHUNKS = 2
CONTRACT_FIRST = (((0,), (0,)), ((), ()))


def bits_of(count):
    return count.bit_length() - 1


def mask_of(step):
    return (1 << step) - 1


def mirror(bit):
    return (2 << bit) - 2


def swap(value, axis, mask):
    count = lax.axis_size(axis)
    return lax.ppermute(value, axis, [(i, i ^ mask) for i in range(count)])


def other(value, axis):
    count = {name: lax.axis_size(name) for name in ("gx", "gy")}
    pairs = []
    for x in range(count["gx"]):
        for y in range(count["gy"]):
            i = x if axis == "gx" else y
            last = count[axis] - 1
            j = (i - 1 if i % 2 == 0 else i + 1) % count[axis]
            if axis == "gx":
                target = (j, y)
            else:
                target = (x ^ 1, y) if i in (0, last) else (x, j)
            pairs.append((x * count["gy"] + y, target[0] * count["gy"] + target[1]))
    return lax.ppermute(value, ("gx", "gy"), pairs)


def relative_block(block, device, steps):
    left = block ^ device
    place = left * 0
    for step in range(steps, 0, -1):
        bit = (left >> (step - 1)) & 1
        place = place | (bit << (steps - step))
        left = left ^ (bit * mask_of(step))
    return place


def halves(value):
    high = value.astype(BF16)
    low = (value - high.astype(F32)).astype(BF16)
    return jnp.concatenate([high, low], axis=1)


def joined(value):
    width = value.shape[1] // 2
    return value[:, :width] + value[:, width:]


def mm(left, right):
    return jnp.dot(left, right, preferred_element_type=F32)


def copies_of(pairs, semaphores):
    copies = [
        pltpu.make_async_copy(source, target, semaphores.at[i])
        for i, (source, target) in enumerate(pairs)
    ]
    for copy in copies:
        copy.start()
    return copies


def terms_kernel(
    steps, rhs_hbm, basis_hbm, ids_hbm, keep_ref, send_ref, low_ref, rhs_ref, basis_ref, ids_ref, sems
):
    device = lax.axis_index("gx")
    subs, functions, _ = basis_ref.shape
    pairs = [(ids_hbm, ids_ref)]
    for s in range(subs):
        pairs += [(basis_hbm.at[s, 0], basis_ref.at[s]), (rhs_hbm.at[s, 0], rhs_ref.at[s])]
    copies = copies_of(pairs, sems)
    half, width = keep_ref.shape
    order = 2 * half
    block = order >> steps
    copies[0].wait()
    ids = jnp.concatenate([ids_ref[s] for s in range(subs)], axis=1)
    row = lax.broadcasted_iota(jnp.int32, (16, ids.shape[1]), 0)
    coded = jnp.where(row == 0, ids // 256, jnp.where(row == 1, ids % 256, 0))
    send_ref[half:] = coded.astype(F32).astype(BF16)
    place = relative_block(ids // block, device, steps) * block + ids % block
    rows = lax.broadcasted_iota(jnp.int32, (order, ids.shape[1]), 0)
    pick = (rows == place).astype(BF16)
    terms = []
    for s in range(subs):
        copies[1 + 2 * s].wait()
        copies[2 + 2 * s].wait()
        value = rhs_ref[s]
        high = value.astype(BF16)
        low = (value - high.astype(F32)).astype(BF16)
        low_ref[s] = high
        terms.append(joined(mm(basis_ref[s], jnp.concatenate([high, low], axis=1))))
    total = joined(mm(pick, halves(jnp.concatenate(terms, axis=0))))
    keep_ref[...] = total[:half]
    send_ref[:half] = total[half:].astype(BF16)


def exchange_kernel(places, keep_ref, got_ref, other_ref, *rest):
    holders, (next_ref, send_ref) = (got_ref, *rest[:-2]), rest[-2:]
    rows = keep_ref.shape[0]
    total = keep_ref[...] + got_ref[:rows].astype(F32)
    next_ref[...] = total
    send_ref[:rows] = total.astype(BF16)
    end = send_ref.shape[0] - other_ref.shape[0]
    row = lax.broadcasted_iota(jnp.int32, (end - rows, keep_ref.shape[1]), 0)
    packed = jnp.zeros(row.shape, F32)
    for q, (holder, start, _) in enumerate(places):
        code = holders[holder][start : start + 16].astype(F32)
        packed = jnp.where(row == 2 * q, code[0:1], packed)
        packed = jnp.where(row == 2 * q + 1, code[1:2], packed)
    send_ref[rows:end] = packed.astype(BF16)
    send_ref[end:] = other_ref[...]


def halve_kernel(known, keep_ref, got_ref, sent_ref, next_ref, send_ref):
    rows = keep_ref.shape[0]
    half = rows // 2
    total = keep_ref[...] + got_ref[:rows].astype(F32)
    next_ref[...] = total[:half]
    send_ref[:half] = total[half:].astype(BF16)
    send_ref[half : half + known] = sent_ref[rows:]
    send_ref[half + known :] = got_ref[rows:]


def join_kernel(near_ref, far_ref, token_ref, out_ref):
    rows = near_ref.shape[0]
    out_ref[:rows] = near_ref[...]
    out_ref[rows:] = far_ref[...]


def sum_kernel(keep_ref, got_ref, *rest):
    halo_refs, next_ref, send_ref = rest[:-2], rest[-2], rest[-1]
    rows = keep_ref.shape[0]
    total = keep_ref[...] + got_ref[:rows].astype(F32)
    next_ref[...] = total
    send_ref[:rows] = total.astype(BF16)
    at = rows
    for ref in halo_refs:
        send_ref[at : at + ref.shape[0]] = ref[...]
        at += ref.shape[0]


def forward_kernel(keep_ref, got_ref, pair_ref, next_ref, send_ref):
    rows = keep_ref.shape[0]
    total = keep_ref[...] + got_ref[:rows].astype(F32)
    next_ref[...] = total
    send_ref[:rows] = total.astype(BF16)
    start = pair_ref.shape[0] - (send_ref.shape[0] - rows)
    send_ref[rows:] = pair_ref[start:]


def outward(width, groups, subs, send_xp, send_xo, send_yp, send_yo):
    even_x = lax.axis_index("gx") % 2 == 0
    even_y = lax.axis_index("gy") % 2 == 0
    west, east = groups(0, 0), groups(subs - 1, 1)
    send_xp[...] = jnp.where(even_x, east, west)
    send_xo[...] = jnp.where(even_x, west, east)
    for s in range(subs):
        south, north = groups(s, 2), groups(s, 3)
        send_yp[s * width : (s + 1) * width] = jnp.where(even_y, north, south)
        send_yo[s * width : (s + 1) * width] = jnp.where(even_y, south, north)


def solve_kernel(width, inverse_ref, rhs_ref, token_ref, own_ref, margin_ref, *sends):
    subs, rows, _ = own_ref.shape
    for s in range(subs):
        value = mm(inverse_ref[s, 0], rhs_ref[s])
        own_ref[s] = value[:rows]
        margin_ref[s] = value[rows:].astype(BF16)

    def groups(sub, number):
        return margin_ref[sub, number * width : (number + 1) * width]

    outward(width, groups, subs, *sends)


def pick_kernel(places, rows_ref, token_ref, *rest):
    id_refs, out_ref = rest[:-1], rest[-1]
    half, order = rows_ref.shape
    width = id_refs[0].shape[1]
    if out_ref.shape[1] > half:
        out_ref[...] = jnp.zeros(out_ref.shape, BF16)
    names = lax.broadcasted_iota(jnp.int32, (order, width), 0)
    rows = rows_ref[...]
    for q, (holder, start, row) in enumerate(places):
        code = id_refs[holder][start : start + 16].astype(F32)[row : row + 2]
        ids = (code[0:1] * 256.0 + code[1:2]).astype(jnp.int32)
        pick = (names == ids).astype(BF16)
        out_ref[q * width : (q + 1) * width, :half] = mm(rows, pick).T.astype(BF16)
    end = len(places) * width
    if out_ref.shape[0] > end:
        carried_ref = id_refs[-1]
        out_ref[end:, : carried_ref.shape[1]] = carried_ref[...]


def arranged(low, masks, first):
    device = lax.axis_index("gy")
    rows = low.shape[0]
    per_device = rows >> len(masks)
    half = rows // 2
    place = lax.broadcasted_iota(jnp.int32, (half, rows), 0) + first
    target = lax.broadcasted_iota(jnp.int32, (half, rows), 1)
    piece = place // per_device
    source = piece * 0 + device
    for bit, mask in enumerate(masks):
        source = source ^ (((piece >> bit) & 1) * mask)
    pick = (source * per_device + place % per_device == target).astype(BF16)
    return mm(pick, low).astype(BF16)


def coarse_kernel(rows, masks, near_ref, far_ref, keep_ref, halo_ref, *rest):
    got_refs, next_ref, send_ref = rest[:-2], rest[-2], rest[-1]
    total = keep_ref[...]
    for ref in got_refs:
        total = total + ref[:rows].astype(F32)
    low = total.astype(BF16)
    half = next_ref.shape[0]
    count = near_ref.shape[0]
    value = mm(near_ref[...], arranged(low, masks, 0))
    value = value + mm(far_ref[:count, : rows // 2], arranged(low, masks, rows // 2))
    next_ref[...] = value[:half]
    send_ref[:half] = value[half:].astype(BF16)
    send_ref[half:] = halo_ref[...]


def halve_halo_kernel(keep_ref, got_ref, halo_ref, next_ref, send_ref):
    rows = keep_ref.shape[0]
    half = rows // 2
    total = keep_ref[...] + got_ref[:rows].astype(F32)
    next_ref[...] = total[:half]
    send_ref[:half] = total[half:].astype(BF16)
    send_ref[half:] = halo_ref[...]


def spread_pick(rows, spill, sides):
    spill = jnp.concatenate([spill[d : d + 1] for d in sides], axis=1)
    iota = lax.broadcasted_iota(jnp.int32, (rows, spill.shape[1]), 0)
    return (iota == spill).astype(BF16)


def west_east(subs, sub, groups, pair, other, even):
    west = groups(sub - 1, 1) if sub > 0 else jnp.where(even, other, pair)
    east = groups(sub + 1, 0) if sub < subs - 1 else jnp.where(even, pair, other)
    return [west, east]


def south_north(sub, width, pair, other, even):
    rows = slice(sub * width, (sub + 1) * width)
    return [jnp.where(even, other[rows], pair[rows]), jnp.where(even, pair[rows], other[rows])]


def other_neighbour(axis):
    device = lax.axis_index(axis)
    even = device % 2 == 0
    other = jnp.where(even, device - 1, device + 1)
    return device, even, other


def from_other(axis, refs, masks, distance):
    device, even, _ = other_neighbour(axis)
    source = jnp.where(even, device - distance, device + distance)
    size, refs = refs
    value = jnp.zeros((size, refs[0].shape[1]), BF16)
    for ref, mask in zip(refs, masks):
        value = jnp.where((device ^ mask) == source, ref[ref.shape[0] - size :], value)
    return even, value


def local_kernel(own_ref, spill_ref, basis_ref, token_ref, far_ref, *rest):
    y_refs, (out_ref, left_ref) = rest[:-2], rest[-2:]
    subs, rows, _ = own_ref.shape
    width = spill_ref.shape[3]
    halo = subs * width
    masks = [mirror(bit) for bit in range(1, len(y_refs))]
    even, other = from_other("gy", (halo, y_refs[1:]), masks, 2)
    pair = far_ref[far_ref.shape[0] - halo :, : own_ref.shape[2]]
    for s in range(subs):
        values = jnp.concatenate(south_north(s, width, pair, other, even), axis=0)
        out_ref[s] = own_ref[s] + mm(spread_pick(rows, spill_ref[s, 0], (2, 3)), values)
        left_ref[s, :, : 2 * width] = spread_pick(rows, spill_ref[s, 0], (0, 1))
        basis = basis_ref[s, 0].astype(F32)
        left_ref[s, :, 2 * width :] = jnp.concatenate([basis, basis], axis=0).T.astype(BF16)


def correction_kernel(width, local_ref, left_ref, margin_ref, operator_ref, keep_ref, *rest):
    x_refs, (out_ref, low_ref, image_ref, *sends) = rest[:-7], rest[-7:]
    subs, rows, columns = local_ref.shape
    functions = keep_ref.shape[0] // subs
    picked = keep_ref[...] + x_refs[-1][: keep_ref.shape[0]].astype(F32)
    masks = [mask_of(step) for step in range(2, len(x_refs) + 1)]
    even, other = from_other("gx", (width, x_refs[1:]), masks, 1)
    pair = x_refs[0][x_refs[0].shape[0] - width :]

    def margins(sub, number):
        return margin_ref[sub, number * width : (number + 1) * width]

    for s in range(subs):
        part = picked[s * functions : (s + 1) * functions]
        high = part.astype(BF16)
        low = (part - high.astype(F32)).astype(BF16)
        values = west_east(subs, s, margins, pair, other, even) + [high, low]
        value = local_ref[s] + mm(left_ref[s], jnp.concatenate(values, axis=0))
        out_ref[s] = value
        low = value.astype(BF16)
        low_ref[s] = low
        image_ref[s] = mm(operator_ref[s, 0, rows:], low).astype(BF16)

    def images(sub, number):
        return image_ref[sub, number * width : (number + 1) * width]

    outward(width, images, subs, *sends)


def image_kernel(
    operator_ref, low_ref, rhs_ref, correction_ref, spill_ref, part_ref, pick_ref, out_ref, sems
):
    subs, rows, _ = low_ref.shape
    copies = copies_of([(correction_ref.at[s], out_ref.at[s, 0]) for s in range(subs)], sems)
    for s in range(subs):
        part_ref[s] = rhs_ref[s, 0] - mm(operator_ref[s, 0, :rows], low_ref[s])
        pick_ref[s] = spread_pick(rows, spill_ref[s, 0], range(4))
    for copy in copies:
        copy.wait()


def inner(axis, value):
    device, count = lax.axis_index(axis), lax.axis_size(axis)
    has = jnp.logical_and(device != 0, device != count - 1)
    return jnp.where(has, value, jnp.zeros(value.shape, value.dtype))


def residual_kernel(
    width, part_ref, image_ref, pick_ref, xp_ref, xo_ref, yp_ref, yo_ref, out_ref, value_ref, sems
):
    subs, rows, _ = part_ref.shape
    even_x = lax.axis_index("gx") % 2 == 0
    even_y = lax.axis_index("gy") % 2 == 0

    def margins(sub, number):
        return image_ref[sub, number * width : (number + 1) * width]

    other_x, other_y = inner("gx", xo_ref[...]), inner("gy", yo_ref[...])
    copies = []
    tile = rows // CHUNKS
    for s in range(subs):
        values = west_east(subs, s, margins, xp_ref[...], other_x, even_x)
        values += south_north(s, width, yp_ref[...], other_y, even_y)
        values = jnp.concatenate(values, axis=0)
        for at in range(0, rows, tile):
            part = slice(at, at + tile)
            value_ref[s, part] = part_ref[s, part] - mm(pick_ref[s, part], values)
            source, target = value_ref.at[s, pl.ds(at, tile)], out_ref.at[s, 0, pl.ds(at, tile)]
            copies.append(pltpu.make_async_copy(source, target, sems.at[len(copies)]))
            copies[-1].start()
    for copy in copies:
        copy.wait()


VMEM = pl.BlockSpec(memory_space=pltpu.VMEM)
HBM = pl.BlockSpec(memory_space=pltpu.HBM)
ANY = pl.BlockSpec(memory_space=pl.ANY)
MIB = 1024 * 1024


def call(kernel, outs, args, name, scratch=(), ins=None, out_specs=None, limit=4, cost=10**9):
    return pl.pallas_call(
        kernel,
        out_shape=[jax.ShapeDtypeStruct(shape, dtype) for shape, dtype in outs],
        in_specs=ins or [VMEM] * len(args),
        out_specs=out_specs or [VMEM] * len(outs),
        scratch_shapes=list(scratch),
        compiler_params=pltpu.CompilerParams(vmem_limit_bytes=limit * MIB),
        cost_estimate=pl.CostEstimate(flops=cost, bytes_accessed=MIB, transcendentals=0),
        name=name,
    )(*args)


def body(
    adjoint_rhs, local_inverse, local_operator, spill_rows, coarse_basis, coarse_ids, coarse_inverse
):
    subs, _, rows, width = adjoint_rhs.shape
    margin = spill_rows.shape[3]
    functions = coarse_ids.shape[2]
    order = coarse_inverse.shape[1]
    count_x, count_y = lax.axis_size("gx"), lax.axis_size("gy")
    steps_x, steps_y = bits_of(count_x), bits_of(count_y)
    listed = subs * functions
    halo = subs * margin
    dma = pltpu.SemaphoreType.DMA
    block = (subs, rows, width)
    messages = [((margin, width), BF16)] * 2 + [((halo, width), BF16)] * 2

    gather_masks = [1 << (steps_y - 1 - i) for i in range(steps_y)]
    near = coarse_inverse
    far = swap(near, "gy", gather_masks[0])

    size = order // 2
    keep, send, low = call(
        functools.partial(terms_kernel, steps_x),
        [((size, width), F32), ((size + 16, listed), BF16), (block, BF16)],
        [pltpu.with_memory_space_constraint(x, pltpu.HBM) for x in (adjoint_rhs, coarse_basis, coarse_ids)],
        "coarse_terms",
        ins=[HBM] * 3,
        scratch=[
            pltpu.VMEM(block, F32),
            pltpu.VMEM((subs, functions, rows), BF16),
            pltpu.VMEM(coarse_ids.shape, jnp.int32),
            dma((1 + 2 * subs,)),
        ],
        limit=12,
    )
    got = swap(send, "gx", mask_of(1))
    id_places = [(send, size, 0)]
    for step in range(2, steps_x + 1):
        half = size // 2
        known = 16 * len(id_places)
        id_places = id_places + [(got, size + 16 * i, 0) for i in range(len(id_places))]
        keep, send = call(
            functools.partial(halve_kernel, known),
            [((half, width), F32), ((half + 2 * known, listed), BF16)],
            [keep, got, send],
            "coarse_halve",
        )
        got = swap(send, "gx", mask_of(step))
        size = half
    id_places = id_places + [(got, size + 16 * i, 0) for i in range(len(id_places))]

    holders, places = [got], []
    for q in range(count_x):
        p = sum(((q >> (steps_x - k)) & 1) << (k - 1) for k in range(1, steps_x + 1))
        array, start, _ = id_places[p]
        found = [i for i, holder in enumerate(holders) if holder is array]
        if not found:
            holders.append(array)
            found = [len(holders) - 1]
        places.append((found[0], start, 0))

    own, margins, halo_xp, halo_xo, halo_yp, halo_yo = call(
        functools.partial(solve_kernel, margin),
        [(block, F32), ((subs, 4 * margin, width), BF16)] + messages,
        [local_inverse, low, send],
        "local_solve",
        ins=[VMEM, VMEM, ANY],
        limit=12,
    )

    def join(near, far, token):
        shape = (2 * near.shape[0], near.shape[1])
        return call(
            join_kernel, [(shape, BF16)], [near, far, token], "inverse_join", ins=[VMEM, VMEM, ANY]
        )[0]

    def picked(value, token, places, holders, *carried):
        rows = count_x * listed
        wide = rows + halo * len(carried)
        return call(
            functools.partial(pick_kernel, places),
            [((wide, max(value.shape[0], width * len(carried))), BF16)],
            [value, token, *holders, *carried],
            "inverse_pick",
            ins=[VMEM, ANY] + [VMEM] * (len(holders) + len(carried)),
            limit=8,
        )[0]

    near = join(near, far, own)
    far = swap(near, "gy", gather_masks[1])

    packed = -(-2 * count_x // 16) * 16
    keep, send = call(
        functools.partial(exchange_kernel, places),
        [((size, width), F32), ((size + packed + halo, width), BF16)],
        [keep, got, halo_yo, *holders[1:]],
        "coarse_sum",
    )
    got = swap(send, "gy", mask_of(1))
    y_got = [got]
    for mask in gather_masks[2:-1]:
        near = join(near, far, got)
        far = swap(near, "gy", mask)
    near = join(near, far, got)
    partner = [(0, size + 2 * q // 16 * 16, 2 * q % 16) for q in range(count_x)]
    far = swap(picked(near, got, partner, [got], halo_yp), "gy", gather_masks[-1])
    pending = [got]
    bit = 1
    while bit < steps_y:
        for extra in pending[1:]:
            keep = keep + extra[:size].astype(F32)
        keep, send = call(
            forward_kernel,
            [((size, width), F32), ((size + halo, width), BF16)],
            [keep, pending[0], y_got[-1]],
            "coarse_sum",
        )
        masks = [1 << bit]
        pending = [swap(send, "gy", mask) for mask in masks]
        y_got += pending
        bit += 1

    near = picked(near, send, places, holders)

    half = count_x * listed // 2
    keep, send = call(
        functools.partial(coarse_kernel, size, gather_masks),
        [((half, width), F32), ((half + margin, width), BF16)],
        [near, far, keep, halo_xp, *pending],
        "coarse_solve",
    )
    x_got = [swap(send, "gx", mask_of(1))]
    for step in range(2, steps_x + 1):
        half = half // 2
        keep, send = call(
            halve_halo_kernel,
            [((half, width), F32), ((half + margin, width), BF16)],
            [keep, x_got[-1], halo_xo],
            "picked_halve",
        )
        x_got.append(swap(send, "gx", mask_of(step)))

    local, left = call(
        local_kernel,
        [(block, F32), ((subs, rows, 2 * margin + 2 * functions), BF16)],
        [own, spill_rows, coarse_basis, send, far, *y_got],
        "local_spread",
        ins=[VMEM] * 3 + [ANY] + [VMEM] * (1 + len(y_got)),
        limit=8,
    )
    correction, low, image, *sends = call(
        functools.partial(correction_kernel, margin),
        [(block, F32), (block, BF16), ((subs, 4 * margin, width), BF16)] + messages,
        [local, left, margins, local_operator, keep, *x_got],
        "correction",
        limit=12,
    )
    got_yo = other(sends[3], "gy")
    got_xo = other(sends[1], "gx")
    got_yp = swap(sends[2], "gy", 1)
    got_xp = swap(sends[0], "gx", 1)

    part, pick, correction = call(
        image_kernel,
        [(block, F32), ((subs, rows, 4 * margin), BF16), (adjoint_rhs.shape, F32)],
        [local_operator, low, adjoint_rhs, correction, spill_rows],
        "image_own",
        out_specs=[VMEM, VMEM, HBM],
        scratch=[dma((subs,))],
        limit=12,
    )
    (residual,) = call(
        functools.partial(residual_kernel, margin),
        [(adjoint_rhs.shape, F32)],
        [part, image, pick, got_xp, got_xo, got_yp, got_yo],
        "residual",
        out_specs=[HBM],
        scratch=[pltpu.VMEM(block, F32), dma((CHUNKS * subs,))],
    )
    return correction, residual


def solution(mesh):
    in_specs = (
        P("gx", "gy", None, None),
        P("gx", "gy", None, None),
        P("gx", "gy", None, None),
        P("gx", "gy", None, None),
        P("gx", "gy", None, None),
        P("gx", "gy", None),
        P(("gx", "gy"), None),
    )
    out_specs = (P("gx", "gy", None, None), P("gx", "gy", None, None))
    return jax.shard_map(body, mesh=mesh, in_specs=in_specs, out_specs=out_specs, check_vma=False)
```

```python
import functools
import jax
import jax.numpy as jnp
from jax import lax
from jax.experimental import pallas as pl
from jax.experimental.pallas import tpu as pltpu
from jax.sharding import PartitionSpec as P

F32 = jnp.float32
BF16 = jnp.bfloat16
CHUNKS = 2
CONTRACT_FIRST = (((0,), (0,)), ((), ()))


def bits_of(count):
    return count.bit_length() - 1


def mask_of(step):
    return (1 << step) - 1


def mirror(bit):
    return (2 << bit) - 2


def swap(value, axis, mask):
    count = lax.axis_size(axis)
    return lax.ppermute(value, axis, [(i, i ^ mask) for i in range(count)])


def other(value, axis):
    count = {name: lax.axis_size(name) for name in ("gx", "gy")}
    pairs = []
    for x in range(count["gx"]):
        for y in range(count["gy"]):
            i = x if axis == "gx" else y
            last = count[axis] - 1
            j = (i - 1 if i % 2 == 0 else i + 1) % count[axis]
            if axis == "gx":
                target = (j, y)
            else:
                target = (x ^ 1, y) if i in (0, last) else (x, j)
            pairs.append((x * count["gy"] + y, target[0] * count["gy"] + target[1]))
    return lax.ppermute(value, ("gx", "gy"), pairs)


def relative_block(block, device, steps):
    left = block ^ device
    place = left * 0
    for step in range(steps, 0, -1):
        bit = (left >> (step - 1)) & 1
        place = place | (bit << (steps - step))
        left = left ^ (bit * mask_of(step))
    return place


def halves(value):
    high = value.astype(BF16)
    low = (value - high.astype(F32)).astype(BF16)
    return jnp.concatenate([high, low], axis=1)


def joined(value):
    width = value.shape[1] // 2
    return value[:, :width] + value[:, width:]


def mm(left, right):
    return jnp.dot(left, right, preferred_element_type=F32)


def copies_of(pairs, semaphores):
    copies = [
        pltpu.make_async_copy(source, target, semaphores.at[i])
        for i, (source, target) in enumerate(pairs)
    ]
    for copy in copies:
        copy.start()
    return copies


def terms_kernel(
    steps, rhs_hbm, basis_hbm, ids_hbm, keep_ref, send_ref, low_ref, rhs_ref, basis_ref, ids_ref, sems
):
    device = lax.axis_index("gx")
    subs, functions, _ = basis_ref.shape
    pairs = [(ids_hbm, ids_ref)]
    for s in range(subs):
        pairs += [(basis_hbm.at[s, 0], basis_ref.at[s]), (rhs_hbm.at[s, 0], rhs_ref.at[s])]
    copies = copies_of(pairs, sems)
    half, width = keep_ref.shape
    order = 2 * half
    block = order >> steps
    copies[0].wait()
    ids = jnp.concatenate([ids_ref[s] for s in range(subs)], axis=1)
    row = lax.broadcasted_iota(jnp.int32, (16, ids.shape[1]), 0)
    coded = jnp.where(row == 0, ids // 256, jnp.where(row == 1, ids % 256, 0))
    send_ref[half:] = coded.astype(F32).astype(BF16)
    place = relative_block(ids // block, device, steps) * block + ids % block
    rows = lax.broadcasted_iota(jnp.int32, (order, ids.shape[1]), 0)
    pick = (rows == place).astype(BF16)
    terms = []
    for s in range(subs):
        copies[1 + 2 * s].wait()
        copies[2 + 2 * s].wait()
        value = rhs_ref[s]
        high = value.astype(BF16)
        low = (value - high.astype(F32)).astype(BF16)
        low_ref[s] = high
        terms.append(joined(mm(basis_ref[s], jnp.concatenate([high, low], axis=1))))
    total = joined(mm(pick, halves(jnp.concatenate(terms, axis=0))))
    keep_ref[...] = total[:half]
    send_ref[:half] = total[half:].astype(BF16)


def exchange_kernel(places, keep_ref, got_ref, *rest):
    holders, (next_ref, send_ref) = (got_ref, *rest[:-2]), rest[-2:]
    rows = keep_ref.shape[0]
    total = keep_ref[...] + got_ref[:rows].astype(F32)
    next_ref[...] = total
    send_ref[:rows] = total.astype(BF16)
    row = lax.broadcasted_iota(jnp.int32, (send_ref.shape[0] - rows, keep_ref.shape[1]), 0)
    packed = jnp.zeros(row.shape, F32)
    for q, (holder, start, _) in enumerate(places):
        code = holders[holder][start : start + 16].astype(F32)
        packed = jnp.where(row == 2 * q, code[0:1], packed)
        packed = jnp.where(row == 2 * q + 1, code[1:2], packed)
    send_ref[rows:] = packed.astype(BF16)


def halve_kernel(known, keep_ref, got_ref, sent_ref, next_ref, send_ref):
    rows = keep_ref.shape[0]
    half = rows // 2
    total = keep_ref[...] + got_ref[:rows].astype(F32)
    next_ref[...] = total[:half]
    send_ref[:half] = total[half:].astype(BF16)
    send_ref[half : half + known] = sent_ref[rows:]
    send_ref[half + known :] = got_ref[rows:]


def join_kernel(near_ref, far_ref, token_ref, out_ref):
    rows = near_ref.shape[0]
    out_ref[:rows] = near_ref[...]
    out_ref[rows:] = far_ref[...]


def sum_kernel(keep_ref, got_ref, *rest):
    halo_refs, next_ref, send_ref = rest[:-2], rest[-2], rest[-1]
    rows = keep_ref.shape[0]
    total = keep_ref[...] + got_ref[:rows].astype(F32)
    next_ref[...] = total
    send_ref[:rows] = total.astype(BF16)
    at = rows
    for ref in halo_refs:
        send_ref[at : at + ref.shape[0]] = ref[...]
        at += ref.shape[0]


def sum_kernel(keep_ref, got_ref, other_ref, next_ref, send_ref, copy_ref):
    rows = keep_ref.shape[0]
    total = keep_ref[...] + got_ref[:rows].astype(F32)
    next_ref[...] = total
    send_ref[...] = total.astype(BF16)
    copy_ref[...] = other_ref[...]


def outward(width, groups, subs, send_xp, send_xo, send_yp, send_yo):
    even_x = lax.axis_index("gx") % 2 == 0
    even_y = lax.axis_index("gy") % 2 == 0
    west, east = groups(0, 0), groups(subs - 1, 1)
    send_xp[...] = jnp.where(even_x, east, west)
    send_xo[...] = jnp.where(even_x, west, east)
    for s in range(subs):
        south, north = groups(s, 2), groups(s, 3)
        send_yp[s * width : (s + 1) * width] = jnp.where(even_y, north, south)
        send_yo[s * width : (s + 1) * width] = jnp.where(even_y, south, north)


def solve_kernel(width, inverse_ref, rhs_ref, token_ref, own_ref, margin_ref, *sends):
    subs, rows, _ = own_ref.shape
    for s in range(subs):
        value = mm(inverse_ref[s, 0], rhs_ref[s])
        own_ref[s] = value[:rows]
        margin_ref[s] = value[rows:].astype(BF16)

    def groups(sub, number):
        return margin_ref[sub, number * width : (number + 1) * width]

    outward(width, groups, subs, *sends)


def pick_kernel(places, rows_ref, token_ref, *rest):
    id_refs, out_ref = rest[:-1], rest[-1]
    half, order = rows_ref.shape
    width = id_refs[0].shape[1]
    if out_ref.shape[1] > half:
        out_ref[...] = jnp.zeros(out_ref.shape, BF16)
    names = lax.broadcasted_iota(jnp.int32, (order, width), 0)
    rows = rows_ref[...]
    for q, (holder, start, row) in enumerate(places):
        code = id_refs[holder][start : start + 16].astype(F32)[row : row + 2]
        ids = (code[0:1] * 256.0 + code[1:2]).astype(jnp.int32)
        pick = (names == ids).astype(BF16)
        out_ref[q * width : (q + 1) * width, :half] = mm(rows, pick).T.astype(BF16)
    end = len(places) * width
    if out_ref.shape[0] > end:
        carried_ref = id_refs[-1]
        out_ref[end:, : carried_ref.shape[1]] = carried_ref[...]


def arranged(low, masks, first):
    device = lax.axis_index("gy")
    rows = low.shape[0]
    per_device = rows >> len(masks)
    half = rows // 2
    place = lax.broadcasted_iota(jnp.int32, (half, rows), 0) + first
    target = lax.broadcasted_iota(jnp.int32, (half, rows), 1)
    piece = place // per_device
    source = piece * 0 + device
    for bit, mask in enumerate(masks):
        source = source ^ (((piece >> bit) & 1) * mask)
    pick = (source * per_device + place % per_device == target).astype(BF16)
    return mm(pick, low).astype(BF16)


def coarse_kernel(rows, masks, near_ref, far_ref, keep_ref, halo_ref, *rest):
    got_refs, next_ref, send_ref = rest[:-2], rest[-2], rest[-1]
    total = keep_ref[...]
    for ref in got_refs:
        total = total + ref[:rows].astype(F32)
    low = total.astype(BF16)
    half = next_ref.shape[0]
    count = near_ref.shape[0]
    value = mm(near_ref[...], arranged(low, masks, 0))
    value = value + mm(far_ref[:count, : rows // 2], arranged(low, masks, rows // 2))
    next_ref[...] = value[:half]
    send_ref[:half] = value[half:].astype(BF16)
    send_ref[half:] = halo_ref[...]


def halve_halo_kernel(keep_ref, got_ref, halo_ref, next_ref, send_ref):
    rows = keep_ref.shape[0]
    half = rows // 2
    total = keep_ref[...] + got_ref[:rows].astype(F32)
    next_ref[...] = total[:half]
    send_ref[:half] = total[half:].astype(BF16)
    send_ref[half:] = halo_ref[...]


def spread_pick(rows, spill, sides):
    spill = jnp.concatenate([spill[d : d + 1] for d in sides], axis=1)
    iota = lax.broadcasted_iota(jnp.int32, (rows, spill.shape[1]), 0)
    return (iota == spill).astype(BF16)


def west_east(subs, sub, groups, pair, other, even):
    west = groups(sub - 1, 1) if sub > 0 else jnp.where(even, other, pair)
    east = groups(sub + 1, 0) if sub < subs - 1 else jnp.where(even, pair, other)
    return [west, east]


def south_north(sub, width, pair, other, even):
    rows = slice(sub * width, (sub + 1) * width)
    return [jnp.where(even, other[rows], pair[rows]), jnp.where(even, pair[rows], other[rows])]


def other_neighbour(axis):
    device = lax.axis_index(axis)
    even = device % 2 == 0
    other = jnp.where(even, device - 1, device + 1)
    return device, even, other


def from_other(axis, refs, masks, distance):
    device, even, _ = other_neighbour(axis)
    source = jnp.where(even, device - distance, device + distance)
    size, refs = refs
    value = jnp.zeros((size, refs[0].shape[1]), BF16)
    for ref, mask in zip(refs, masks):
        value = jnp.where((device ^ mask) == source, ref[ref.shape[0] - size :], value)
    return even, value


def inner(axis, value):
    device, count = lax.axis_index(axis), lax.axis_size(axis)
    has = jnp.logical_and(device != 0, device != count - 1)
    return jnp.where(has, value, jnp.zeros(value.shape, value.dtype))


def local_kernel(own_ref, spill_ref, basis_ref, token_ref, far_ref, other_ref, out_ref, left_ref):
    subs, rows, _ = own_ref.shape
    width = spill_ref.shape[3]
    halo = subs * width
    even, other = lax.axis_index("gy") % 2 == 0, inner("gy", other_ref[...])
    pair = far_ref[far_ref.shape[0] - halo :, : own_ref.shape[2]]
    for s in range(subs):
        values = jnp.concatenate(south_north(s, width, pair, other, even), axis=0)
        out_ref[s] = own_ref[s] + mm(spread_pick(rows, spill_ref[s, 0], (2, 3)), values)
        left_ref[s, :, : 2 * width] = spread_pick(rows, spill_ref[s, 0], (0, 1))
        basis = basis_ref[s, 0].astype(F32)
        left_ref[s, :, 2 * width :] = jnp.concatenate([basis, basis], axis=0).T.astype(BF16)


def correction_kernel(width, local_ref, left_ref, margin_ref, operator_ref, keep_ref, *rest):
    x_refs, (out_ref, low_ref, image_ref, *sends) = rest[:-7], rest[-7:]
    subs, rows, columns = local_ref.shape
    functions = keep_ref.shape[0] // subs
    picked = keep_ref[...] + x_refs[-1][: keep_ref.shape[0]].astype(F32)
    masks = [mask_of(step) for step in range(2, len(x_refs) + 1)]
    even, other = from_other("gx", (width, x_refs[1:]), masks, 1)
    pair = x_refs[0][x_refs[0].shape[0] - width :]

    def margins(sub, number):
        return margin_ref[sub, number * width : (number + 1) * width]

    for s in range(subs):
        part = picked[s * functions : (s + 1) * functions]
        high = part.astype(BF16)
        low = (part - high.astype(F32)).astype(BF16)
        values = west_east(subs, s, margins, pair, other, even) + [high, low]
        value = local_ref[s] + mm(left_ref[s], jnp.concatenate(values, axis=0))
        out_ref[s] = value
        low = value.astype(BF16)
        low_ref[s] = low
        image_ref[s] = mm(operator_ref[s, 0, rows:], low).astype(BF16)

    def images(sub, number):
        return image_ref[sub, number * width : (number + 1) * width]

    outward(width, images, subs, *sends)


def image_kernel(
    operator_ref, low_ref, rhs_ref, correction_ref, spill_ref, part_ref, pick_ref, out_ref, sems
):
    subs, rows, _ = low_ref.shape
    copies = copies_of([(correction_ref.at[s], out_ref.at[s, 0]) for s in range(subs)], sems)
    for s in range(subs):
        part_ref[s] = rhs_ref[s, 0] - mm(operator_ref[s, 0, :rows], low_ref[s])
        pick_ref[s] = spread_pick(rows, spill_ref[s, 0], range(4))
    for copy in copies:
        copy.wait()


def residual_kernel(
    width, part_ref, image_ref, pick_ref, xp_ref, xo_ref, yp_ref, yo_ref, out_ref, value_ref, sems
):
    subs, rows, _ = part_ref.shape
    even_x = lax.axis_index("gx") % 2 == 0
    even_y = lax.axis_index("gy") % 2 == 0

    def margins(sub, number):
        return image_ref[sub, number * width : (number + 1) * width]

    other_x, other_y = inner("gx", xo_ref[...]), inner("gy", yo_ref[...])
    copies = []
    tile = rows // CHUNKS
    for s in range(subs):
        values = west_east(subs, s, margins, xp_ref[...], other_x, even_x)
        values += south_north(s, width, yp_ref[...], other_y, even_y)
        values = jnp.concatenate(values, axis=0)
        for at in range(0, rows, tile):
            part = slice(at, at + tile)
            value_ref[s, part] = part_ref[s, part] - mm(pick_ref[s, part], values)
            source, target = value_ref.at[s, pl.ds(at, tile)], out_ref.at[s, 0, pl.ds(at, tile)]
            copies.append(pltpu.make_async_copy(source, target, sems.at[len(copies)]))
            copies[-1].start()
    for copy in copies:
        copy.wait()


VMEM = pl.BlockSpec(memory_space=pltpu.VMEM)
HBM = pl.BlockSpec(memory_space=pltpu.HBM)
ANY = pl.BlockSpec(memory_space=pl.ANY)
MIB = 1024 * 1024


def call(kernel, outs, args, name, scratch=(), ins=None, out_specs=None, limit=4, cost=10**9):
    return pl.pallas_call(
        kernel,
        out_shape=[jax.ShapeDtypeStruct(shape, dtype) for shape, dtype in outs],
        in_specs=ins or [VMEM] * len(args),
        out_specs=out_specs or [VMEM] * len(outs),
        scratch_shapes=list(scratch),
        compiler_params=pltpu.CompilerParams(vmem_limit_bytes=limit * MIB),
        cost_estimate=pl.CostEstimate(flops=cost, bytes_accessed=MIB, transcendentals=0),
        name=name,
    )(*args)


def body(
    adjoint_rhs, local_inverse, local_operator, spill_rows, coarse_basis, coarse_ids, coarse_inverse
):
    subs, _, rows, width = adjoint_rhs.shape
    margin = spill_rows.shape[3]
    functions = coarse_ids.shape[2]
    order = coarse_inverse.shape[1]
    count_x, count_y = lax.axis_size("gx"), lax.axis_size("gy")
    steps_x, steps_y = bits_of(count_x), bits_of(count_y)
    listed = subs * functions
    halo = subs * margin
    dma = pltpu.SemaphoreType.DMA
    block = (subs, rows, width)
    messages = [((margin, width), BF16)] * 2 + [((halo, width), BF16)] * 2

    gather_masks = [1 << (steps_y - 1 - i) for i in range(steps_y)]
    near = coarse_inverse
    far = swap(near, "gy", gather_masks[0])

    size = order // 2
    keep, send, low = call(
        functools.partial(terms_kernel, steps_x),
        [((size, width), F32), ((size + 16, listed), BF16), (block, BF16)],
        [pltpu.with_memory_space_constraint(x, pltpu.HBM) for x in (adjoint_rhs, coarse_basis, coarse_ids)],
        "coarse_terms",
        ins=[HBM] * 3,
        scratch=[
            pltpu.VMEM(block, F32),
            pltpu.VMEM((subs, functions, rows), BF16),
            pltpu.VMEM(coarse_ids.shape, jnp.int32),
            dma((1 + 2 * subs,)),
        ],
        limit=12,
    )
    got = swap(send, "gx", mask_of(1))
    id_places = [(send, size, 0)]
    for step in range(2, steps_x + 1):
        half = size // 2
        known = 16 * len(id_places)
        id_places = id_places + [(got, size + 16 * i, 0) for i in range(len(id_places))]
        keep, send = call(
            functools.partial(halve_kernel, known),
            [((half, width), F32), ((half + 2 * known, listed), BF16)],
            [keep, got, send],
            "coarse_halve",
        )
        got = swap(send, "gx", mask_of(step))
        size = half
    id_places = id_places + [(got, size + 16 * i, 0) for i in range(len(id_places))]

    holders, places = [got], []
    for q in range(count_x):
        p = sum(((q >> (steps_x - k)) & 1) << (k - 1) for k in range(1, steps_x + 1))
        array, start, _ = id_places[p]
        found = [i for i, holder in enumerate(holders) if holder is array]
        if not found:
            holders.append(array)
            found = [len(holders) - 1]
        places.append((found[0], start, 0))

    own, margins, halo_xp, halo_xo, halo_yp, halo_yo = call(
        functools.partial(solve_kernel, margin),
        [(block, F32), ((subs, 4 * margin, width), BF16)] + messages,
        [local_inverse, low, send],
        "local_solve",
        ins=[VMEM, VMEM, ANY],
        limit=12,
    )

    def join(near, far, token):
        shape = (2 * near.shape[0], near.shape[1])
        return call(
            join_kernel, [(shape, BF16)], [near, far, token], "inverse_join", ins=[VMEM, VMEM, ANY]
        )[0]

    def picked(value, token, places, holders, *carried):
        rows = count_x * listed
        wide = rows + halo * len(carried)
        return call(
            functools.partial(pick_kernel, places),
            [((wide, max(value.shape[0], width * len(carried))), BF16)],
            [value, token, *holders, *carried],
            "inverse_pick",
            ins=[VMEM, ANY] + [VMEM] * (len(holders) + len(carried)),
            limit=8,
        )[0]

    near = join(near, far, own)
    far = swap(near, "gy", gather_masks[1])

    packed = -(-2 * count_x // 16) * 16
    keep, send = call(
        functools.partial(exchange_kernel, places),
        [((size, width), F32), ((size + packed, width), BF16)],
        [keep, got, *holders[1:]],
        "coarse_sum",
    )
    got = swap(send, "gy", mask_of(1))
    for mask in gather_masks[2:-1]:
        near = join(near, far, got)
        far = swap(near, "gy", mask)
    near = join(near, far, got)
    partner = [(0, size + 2 * q // 16 * 16, 2 * q % 16) for q in range(count_x)]
    far = swap(picked(near, got, partner, [got], halo_yp), "gy", gather_masks[-1])
    for bit in range(1, steps_y):
        keep, send, halo_yo = call(
            sum_kernel,
            [((size, width), F32), ((size, width), BF16), ((halo, width), BF16)],
            [keep, got, halo_yo],
            "coarse_sum",
        )
        got = swap(send, "gy", 1 << bit)
    far_halo = other(halo_yo, "gy")

    near = picked(near, send, places, holders)

    half = count_x * listed // 2
    keep, send = call(
        functools.partial(coarse_kernel, size, gather_masks),
        [((half, width), F32), ((half + margin, width), BF16)],
        [near, far, keep, halo_xp, got],
        "coarse_solve",
    )
    x_got = [swap(send, "gx", mask_of(1))]
    for step in range(2, steps_x + 1):
        half = half // 2
        keep, send = call(
            halve_halo_kernel,
            [((half, width), F32), ((half + margin, width), BF16)],
            [keep, x_got[-1], halo_xo],
            "picked_halve",
        )
        x_got.append(swap(send, "gx", mask_of(step)))

    local, left = call(
        local_kernel,
        [(block, F32), ((subs, rows, 2 * margin + 2 * functions), BF16)],
        [own, spill_rows, coarse_basis, send, far, far_halo],
        "local_spread",
        ins=[VMEM] * 3 + [ANY] + [VMEM] * 2,
        limit=8,
    )
    correction, low, image, *sends = call(
        functools.partial(correction_kernel, margin),
        [(block, F32), (block, BF16), ((subs, 4 * margin, width), BF16)] + messages,
        [local, left, margins, local_operator, keep, *x_got],
        "correction",
        limit=12,
    )
    got_yo = other(sends[3], "gy")
    got_xo = other(sends[1], "gx")
    got_yp = swap(sends[2], "gy", 1)
    got_xp = swap(sends[0], "gx", 1)

    part, pick, correction = call(
        image_kernel,
        [(block, F32), ((subs, rows, 4 * margin), BF16), (adjoint_rhs.shape, F32)],
        [local_operator, low, adjoint_rhs, correction, spill_rows],
        "image_own",
        out_specs=[VMEM, VMEM, HBM],
        scratch=[dma((subs,))],
        limit=12,
    )
    (residual,) = call(
        functools.partial(residual_kernel, margin),
        [(adjoint_rhs.shape, F32)],
        [part, image, pick, got_xp, got_xo, got_yp, got_yo],
        "residual",
        out_specs=[HBM],
        scratch=[pltpu.VMEM(block, F32), dma((CHUNKS * subs,))],
    )
    return correction, residual


def solution(mesh):
    in_specs = (
        P("gx", "gy", None, None),
        P("gx", "gy", None, None),
        P("gx", "gy", None, None),
        P("gx", "gy", None, None),
        P("gx", "gy", None, None),
        P("gx", "gy", None),
        P(("gx", "gy"), None),
    )
    out_specs = (P("gx", "gy", None, None), P("gx", "gy", None, None))
    return jax.shard_map(body, mesh=mesh, in_specs=in_specs, out_specs=out_specs, check_vma=False)
```

```python
import functools
import jax
import jax.numpy as jnp
from jax import lax
from jax.experimental import pallas as pl
from jax.experimental.pallas import tpu as pltpu
from jax.sharding import PartitionSpec as P

F32 = jnp.float32
BF16 = jnp.bfloat16
CHUNKS = 2
CONTRACT_FIRST = (((0,), (0,)), ((), ()))


def bits_of(count):
    return count.bit_length() - 1


def mask_of(step):
    return (1 << step) - 1


def mirror(bit):
    return (2 << bit) - 2


def swap(value, axis, mask):
    count = lax.axis_size(axis)
    return lax.ppermute(value, axis, [(i, i ^ mask) for i in range(count)])


def other(value, axis):
    count = {name: lax.axis_size(name) for name in ("gx", "gy")}
    pairs = []
    for x in range(count["gx"]):
        for y in range(count["gy"]):
            i = x if axis == "gx" else y
            last = count[axis] - 1
            j = (i - 1 if i % 2 == 0 else i + 1) % count[axis]
            if axis == "gx":
                target = (j, y)
            else:
                target = (x ^ 1, y) if i in (0, last) else (x, j)
            pairs.append((x * count["gy"] + y, target[0] * count["gy"] + target[1]))
    return lax.ppermute(value, ("gx", "gy"), pairs)


def relative_block(block, device, steps):
    left = block ^ device
    place = left * 0
    for step in range(steps, 0, -1):
        bit = (left >> (step - 1)) & 1
        place = place | (bit << (steps - step))
        left = left ^ (bit * mask_of(step))
    return place


def gathered_place(row, rows, steps):
    per_device = rows >> steps
    left = (row // per_device) ^ lax.axis_index("gy")
    place = row % per_device
    for bit in range(steps):
        place = place + ((left >> bit) & 1) * (rows >> (bit + 1))
    return place


def regathered(value, bit):
    part = value.shape[0] >> (bit + 1)
    pieces = [value[i * part : (i + 1) * part] for i in range(2 << bit)]
    return jnp.concatenate([pieces[i ^ 1] for i in range(2 << bit)], axis=0)


def halves(value):
    high = value.astype(BF16)
    low = (value - high.astype(F32)).astype(BF16)
    return jnp.concatenate([high, low], axis=1)


def joined(value):
    width = value.shape[1] // 2
    return value[:, :width] + value[:, width:]


def mm(left, right):
    return jnp.dot(left, right, preferred_element_type=F32)


def copies_of(pairs, semaphores):
    copies = [
        pltpu.make_async_copy(source, target, semaphores.at[i])
        for i, (source, target) in enumerate(pairs)
    ]
    for copy in copies:
        copy.start()
    return copies


def terms_kernel(
    steps, steps_y, rhs_hbm, basis_hbm, ids_hbm, keep_ref, send_ref, low_ref, rhs_ref, basis_ref, ids_ref, sems
):
    device = lax.axis_index("gx")
    subs, functions, _ = basis_ref.shape
    pairs = [(ids_hbm, ids_ref)]
    for s in range(subs):
        pairs += [(basis_hbm.at[s, 0], basis_ref.at[s]), (rhs_hbm.at[s, 0], rhs_ref.at[s])]
    copies = copies_of(pairs, sems)
    half, width = keep_ref.shape
    order = 2 * half
    block = order >> steps
    copies[0].wait()
    ids = jnp.concatenate([ids_ref[s] for s in range(subs)], axis=1)
    row = lax.broadcasted_iota(jnp.int32, (16, ids.shape[1]), 0)
    coded = jnp.where(row == 0, ids // 256, jnp.where(row == 1, ids % 256, 0))
    send_ref[half:] = coded.astype(F32).astype(BF16)
    place = relative_block(ids // block, device, steps) * block
    place = place + gathered_place(ids % block, block, steps_y)
    rows = lax.broadcasted_iota(jnp.int32, (order, ids.shape[1]), 0)
    pick = (rows == place).astype(BF16)
    terms = []
    for s in range(subs):
        copies[1 + 2 * s].wait()
        copies[2 + 2 * s].wait()
        value = rhs_ref[s]
        high = value.astype(BF16)
        low = (value - high.astype(F32)).astype(BF16)
        low_ref[s] = high
        terms.append(joined(mm(basis_ref[s], jnp.concatenate([high, low], axis=1))))
    terms = jnp.concatenate(terms, axis=0)
    high = terms.astype(BF16)
    low = (terms - high.astype(F32)).astype(BF16)
    total = mm(jnp.concatenate([pick, pick], axis=1), jnp.concatenate([high, low], axis=0))
    keep_ref[...] = total[:half]
    send_ref[:half] = total[half:].astype(BF16)


def exchange_kernel(places, keep_ref, got_ref, *rest):
    holders, (next_ref, send_ref) = (got_ref, *rest[:-2]), rest[-2:]
    rows = keep_ref.shape[0]
    total = keep_ref[...] + got_ref[:rows].astype(F32)
    next_ref[...] = total
    send_ref[:rows] = total.astype(BF16)
    row = lax.broadcasted_iota(jnp.int32, (send_ref.shape[0] - rows, keep_ref.shape[1]), 0)
    packed = jnp.zeros(row.shape, F32)
    for q, (holder, start, _) in enumerate(places):
        code = holders[holder][start : start + 16].astype(F32)
        packed = jnp.where(row == 2 * q, code[0:1], packed)
        packed = jnp.where(row == 2 * q + 1, code[1:2], packed)
    send_ref[rows:] = packed.astype(BF16)


def halve_kernel(known, keep_ref, got_ref, sent_ref, next_ref, send_ref):
    rows = keep_ref.shape[0]
    half = rows // 2
    total = keep_ref[...] + got_ref[:rows].astype(F32)
    next_ref[...] = total[:half]
    send_ref[:half] = total[half:].astype(BF16)
    send_ref[half : half + known] = sent_ref[rows:]
    send_ref[half + known :] = got_ref[rows:]


def join_kernel(near_ref, far_ref, token_ref, out_ref):
    rows = near_ref.shape[0]
    out_ref[:rows] = near_ref[...]
    out_ref[rows:] = far_ref[...]


def sum_kernel(keep_ref, got_ref, *rest):
    halo_refs, next_ref, send_ref = rest[:-2], rest[-2], rest[-1]
    rows = keep_ref.shape[0]
    total = keep_ref[...] + got_ref[:rows].astype(F32)
    next_ref[...] = total
    send_ref[:rows] = total.astype(BF16)
    at = rows
    for ref in halo_refs:
        send_ref[at : at + ref.shape[0]] = ref[...]
        at += ref.shape[0]


def sum_kernel(bit, keep_ref, got_ref, other_ref, next_ref, send_ref, copy_ref):
    rows = keep_ref.shape[0]
    total = keep_ref[...] + regathered(got_ref[:rows].astype(F32), bit)
    next_ref[...] = total
    send_ref[...] = total.astype(BF16)
    copy_ref[...] = other_ref[...]


def outward(width, groups, subs, send_xp, send_xo, send_yp, send_yo):
    even_x = lax.axis_index("gx") % 2 == 0
    even_y = lax.axis_index("gy") % 2 == 0
    west, east = groups(0, 0), groups(subs - 1, 1)
    send_xp[...] = jnp.where(even_x, east, west)
    send_xo[...] = jnp.where(even_x, west, east)
    for s in range(subs):
        south, north = groups(s, 2), groups(s, 3)
        send_yp[s * width : (s + 1) * width] = jnp.where(even_y, north, south)
        send_yo[s * width : (s + 1) * width] = jnp.where(even_y, south, north)


def solve_kernel(width, inverse_ref, rhs_ref, token_ref, own_ref, margin_ref, *sends):
    subs, rows, _ = own_ref.shape
    for s in range(subs):
        value = mm(inverse_ref[s, 0], rhs_ref[s])
        own_ref[s] = value[:rows]
        margin_ref[s] = value[rows:].astype(BF16)

    def groups(sub, number):
        return margin_ref[sub, number * width : (number + 1) * width]

    outward(width, groups, subs, *sends)


def pick_kernel(places, rows_ref, token_ref, *rest):
    id_refs, out_ref = rest[:-1], rest[-1]
    half, order = rows_ref.shape
    width = id_refs[0].shape[1]
    if out_ref.shape[1] > half:
        out_ref[...] = jnp.zeros(out_ref.shape, BF16)
    names = lax.broadcasted_iota(jnp.int32, (order, width), 0)
    rows = rows_ref[...]
    for q, (holder, start, row) in enumerate(places):
        code = id_refs[holder][start : start + 16].astype(F32)[row : row + 2]
        ids = (code[0:1] * 256.0 + code[1:2]).astype(jnp.int32)
        pick = (names == ids).astype(BF16)
        out_ref[q * width : (q + 1) * width, :half] = mm(rows, pick).T.astype(BF16)
    end = len(places) * width
    if out_ref.shape[0] > end:
        carried_ref = id_refs[-1]
        out_ref[end:, : carried_ref.shape[1]] = carried_ref[...]


def coarse_kernel(bit, near_ref, far_ref, keep_ref, halo_ref, got_ref, next_ref, send_ref):
    rows = keep_ref.shape[0]
    total = keep_ref[...] + regathered(got_ref[...].astype(F32), bit)
    low = total.astype(BF16)
    half = next_ref.shape[0]
    count = near_ref.shape[0]
    left = jnp.concatenate([near_ref[...], far_ref[:count, : rows // 2]], axis=1)
    value = mm(left, low)
    next_ref[...] = value[:half]
    send_ref[:half] = value[half:].astype(BF16)
    send_ref[half:] = halo_ref[...]


def halve_halo_kernel(keep_ref, got_ref, halo_ref, next_ref, send_ref):
    rows = keep_ref.shape[0]
    half = rows // 2
    total = keep_ref[...] + got_ref[:rows].astype(F32)
    next_ref[...] = total[:half]
    send_ref[:half] = total[half:].astype(BF16)
    send_ref[half:] = halo_ref[...]


def spread_pick(rows, spill, sides):
    spill = jnp.concatenate([spill[d : d + 1] for d in sides], axis=1)
    iota = lax.broadcasted_iota(jnp.int32, (rows, spill.shape[1]), 0)
    return (iota == spill).astype(BF16)


def west_east(subs, sub, groups, pair, other, even):
    west = groups(sub - 1, 1) if sub > 0 else jnp.where(even, other, pair)
    east = groups(sub + 1, 0) if sub < subs - 1 else jnp.where(even, pair, other)
    return [west, east]


def south_north(sub, width, pair, other, even):
    rows = slice(sub * width, (sub + 1) * width)
    return [jnp.where(even, other[rows], pair[rows]), jnp.where(even, pair[rows], other[rows])]


def other_neighbour(axis):
    device = lax.axis_index(axis)
    even = device % 2 == 0
    other = jnp.where(even, device - 1, device + 1)
    return device, even, other


def from_other(axis, refs, masks, distance):
    device, even, _ = other_neighbour(axis)
    source = jnp.where(even, device - distance, device + distance)
    size, refs = refs
    value = jnp.zeros((size, refs[0].shape[1]), BF16)
    for ref, mask in zip(refs, masks):
        value = jnp.where((device ^ mask) == source, ref[ref.shape[0] - size :], value)
    return even, value


def inner(axis, value):
    device, count = lax.axis_index(axis), lax.axis_size(axis)
    has = jnp.logical_and(device != 0, device != count - 1)
    return jnp.where(has, value, jnp.zeros(value.shape, value.dtype))


def local_kernel(own_ref, spill_ref, basis_ref, token_ref, far_ref, out_ref, left_ref):
    subs, rows, _ = own_ref.shape
    width = spill_ref.shape[3]
    halo = subs * width
    even = lax.axis_index("gy") % 2 == 0
    pair = far_ref[far_ref.shape[0] - halo :, : own_ref.shape[2]]
    for s in range(subs):
        spill = spill_ref[s, 0]
        near = jnp.where(even, spill[3:4], spill[2:3])
        value = pair[s * width : (s + 1) * width]
        out_ref[s] = own_ref[s] + mm(spread_pick(rows, near, (0,)), value)
        left_ref[s, :, : 2 * width] = spread_pick(rows, spill, (0, 1))
        far = jnp.where(even, spill[2:3], spill[3:4])
        basis = basis_ref[s, 0].astype(F32)
        basis = jnp.concatenate([basis, basis], axis=0).T.astype(BF16)
        left_ref[s, :, 2 * width :] = jnp.concatenate([spread_pick(rows, far, (0,)), basis], axis=1)


def correction_kernel(width, local_ref, left_ref, margin_ref, operator_ref, far_ref, keep_ref, *rest):
    x_refs, (out_ref, low_ref, image_ref, *sends) = rest[:-7], rest[-7:]
    subs, rows, columns = local_ref.shape
    functions = keep_ref.shape[0] // subs
    picked = keep_ref[...] + x_refs[-1][: keep_ref.shape[0]].astype(F32)
    masks = [mask_of(step) for step in range(2, len(x_refs) + 1)]
    even, other = from_other("gx", (width, x_refs[1:]), masks, 1)
    pair = x_refs[0][x_refs[0].shape[0] - width :]
    far = inner("gy", far_ref[...])

    def margins(sub, number):
        return margin_ref[sub, number * width : (number + 1) * width]

    for s in range(subs):
        part = picked[s * functions : (s + 1) * functions]
        high = part.astype(BF16)
        low = (part - high.astype(F32)).astype(BF16)
        values = west_east(subs, s, margins, pair, other, even)
        values += [far[s * width : (s + 1) * width], high, low]
        value = local_ref[s] + mm(left_ref[s], jnp.concatenate(values, axis=0))
        out_ref[s] = value
        low = value.astype(BF16)
        low_ref[s] = low
        image_ref[s] = mm(operator_ref[s, 0, rows:], low).astype(BF16)

    def images(sub, number):
        return image_ref[sub, number * width : (number + 1) * width]

    outward(width, images, subs, *sends)


def image_kernel(
    operator_ref, low_ref, rhs_ref, correction_ref, spill_ref, part_ref, pick_ref, out_ref, sems
):
    subs, rows, _ = low_ref.shape
    copies = copies_of([(correction_ref.at[s], out_ref.at[s, 0]) for s in range(subs)], sems)
    for s in range(subs):
        part_ref[s] = rhs_ref[s, 0] - mm(operator_ref[s, 0, :rows], low_ref[s])
        pick_ref[s] = spread_pick(rows, spill_ref[s, 0], range(4))
    for copy in copies:
        copy.wait()


def residual_kernel(
    width, part_ref, image_ref, pick_ref, xp_ref, xo_ref, yp_ref, yo_ref, out_ref, value_ref, sems
):
    subs, rows, _ = part_ref.shape
    even_x = lax.axis_index("gx") % 2 == 0
    even_y = lax.axis_index("gy") % 2 == 0

    def margins(sub, number):
        return image_ref[sub, number * width : (number + 1) * width]

    other_x, other_y = inner("gx", xo_ref[...]), inner("gy", yo_ref[...])
    copies = []
    tile = rows // CHUNKS
    for s in range(subs):
        values = west_east(subs, s, margins, xp_ref[...], other_x, even_x)
        values += south_north(s, width, yp_ref[...], other_y, even_y)
        values = jnp.concatenate(values, axis=0)
        for at in range(0, rows, tile):
            part = slice(at, at + tile)
            value_ref[s, part] = part_ref[s, part] - mm(pick_ref[s, part], values)
            source, target = value_ref.at[s, pl.ds(at, tile)], out_ref.at[s, 0, pl.ds(at, tile)]
            copies.append(pltpu.make_async_copy(source, target, sems.at[len(copies)]))
            copies[-1].start()
    for copy in copies:
        copy.wait()


VMEM = pl.BlockSpec(memory_space=pltpu.VMEM)
HBM = pl.BlockSpec(memory_space=pltpu.HBM)
ANY = pl.BlockSpec(memory_space=pl.ANY)
MIB = 1024 * 1024


def call(kernel, outs, args, name, scratch=(), ins=None, out_specs=None, limit=4, cost=10**9):
    return pl.pallas_call(
        kernel,
        out_shape=[jax.ShapeDtypeStruct(shape, dtype) for shape, dtype in outs],
        in_specs=ins or [VMEM] * len(args),
        out_specs=out_specs or [VMEM] * len(outs),
        scratch_shapes=list(scratch),
        compiler_params=pltpu.CompilerParams(vmem_limit_bytes=limit * MIB),
        cost_estimate=pl.CostEstimate(flops=cost, bytes_accessed=MIB, transcendentals=0),
        name=name,
    )(*args)


def body(
    adjoint_rhs, local_inverse, local_operator, spill_rows, coarse_basis, coarse_ids, coarse_inverse
):
    subs, _, rows, width = adjoint_rhs.shape
    margin = spill_rows.shape[3]
    functions = coarse_ids.shape[2]
    order = coarse_inverse.shape[1]
    count_x, count_y = lax.axis_size("gx"), lax.axis_size("gy")
    steps_x, steps_y = bits_of(count_x), bits_of(count_y)
    listed = subs * functions
    halo = subs * margin
    dma = pltpu.SemaphoreType.DMA
    block = (subs, rows, width)
    messages = [((margin, width), BF16)] * 2 + [((halo, width), BF16)] * 2

    gather_masks = [1 << (steps_y - 1 - i) for i in range(steps_y)]
    near = coarse_inverse
    far = swap(near, "gy", gather_masks[0])

    size = order // 2
    keep, send, low = call(
        functools.partial(terms_kernel, steps_x, steps_y),
        [((size, width), F32), ((size + 16, listed), BF16), (block, BF16)],
        [pltpu.with_memory_space_constraint(x, pltpu.HBM) for x in (adjoint_rhs, coarse_basis, coarse_ids)],
        "coarse_terms",
        ins=[HBM] * 3,
        scratch=[
            pltpu.VMEM(block, F32),
            pltpu.VMEM((subs, functions, rows), BF16),
            pltpu.VMEM(coarse_ids.shape, jnp.int32),
            dma((1 + 2 * subs,)),
        ],
        limit=12,
    )
    got = swap(send, "gx", mask_of(1))
    id_places = [(send, size, 0)]
    for step in range(2, steps_x + 1):
        half = size // 2
        known = 16 * len(id_places)
        id_places = id_places + [(got, size + 16 * i, 0) for i in range(len(id_places))]
        keep, send = call(
            functools.partial(halve_kernel, known),
            [((half, width), F32), ((half + 2 * known, listed), BF16)],
            [keep, got, send],
            "coarse_halve",
        )
        got = swap(send, "gx", mask_of(step))
        size = half
    id_places = id_places + [(got, size + 16 * i, 0) for i in range(len(id_places))]

    holders, places = [got], []
    for q in range(count_x):
        p = sum(((q >> (steps_x - k)) & 1) << (k - 1) for k in range(1, steps_x + 1))
        array, start, _ = id_places[p]
        found = [i for i, holder in enumerate(holders) if holder is array]
        if not found:
            holders.append(array)
            found = [len(holders) - 1]
        places.append((found[0], start, 0))

    own, margins, halo_xp, halo_xo, halo_yp, halo_yo = call(
        functools.partial(solve_kernel, margin),
        [(block, F32), ((subs, 4 * margin, width), BF16)] + messages,
        [local_inverse, low, send],
        "local_solve",
        ins=[VMEM, VMEM, ANY],
        limit=12,
    )

    def join(near, far, token):
        shape = (2 * near.shape[0], near.shape[1])
        return call(
            join_kernel, [(shape, BF16)], [near, far, token], "inverse_join", ins=[VMEM, VMEM, ANY]
        )[0]

    def picked(value, token, places, holders, *carried):
        rows = count_x * listed
        wide = rows + halo * len(carried)
        return call(
            functools.partial(pick_kernel, places),
            [((wide, max(value.shape[0], width * len(carried))), BF16)],
            [value, token, *holders, *carried],
            "inverse_pick",
            ins=[VMEM, ANY] + [VMEM] * (len(holders) + len(carried)),
            limit=8,
        )[0]

    near = join(near, far, own)
    far = swap(near, "gy", gather_masks[1])

    packed = -(-2 * count_x // 16) * 16
    keep, send = call(
        functools.partial(exchange_kernel, places),
        [((size, width), F32), ((size + packed, width), BF16)],
        [keep, got, *holders[1:]],
        "coarse_sum",
    )
    got = swap(send, "gy", mask_of(1))
    for mask in gather_masks[2:-1]:
        near = join(near, far, got)
        far = swap(near, "gy", mask)
    near = join(near, far, got)
    partner = [(0, size + 2 * q // 16 * 16, 2 * q % 16) for q in range(count_x)]
    far = swap(picked(near, got, partner, [got], halo_yp), "gy", gather_masks[-1])
    for bit in range(1, steps_y):
        keep, send, halo_yo = call(
            functools.partial(sum_kernel, bit - 1),
            [((size, width), F32), ((size, width), BF16), ((halo, width), BF16)],
            [keep, got, halo_yo],
            "coarse_sum",
        )
        got = swap(send, "gy", 1 << bit)
    far_halo = other(halo_yo, "gy")

    near = picked(near, send, places, holders)

    half = count_x * listed // 2
    keep, send = call(
        functools.partial(coarse_kernel, steps_y - 1),
        [((half, width), F32), ((half + margin, width), BF16)],
        [near, far, keep, halo_xp, got],
        "coarse_solve",
    )
    x_got = [swap(send, "gx", mask_of(1))]
    for step in range(2, steps_x + 1):
        half = half // 2
        keep, send = call(
            halve_halo_kernel,
            [((half, width), F32), ((half + margin, width), BF16)],
            [keep, x_got[-1], halo_xo],
            "picked_halve",
        )
        x_got.append(swap(send, "gx", mask_of(step)))

    local, left = call(
        local_kernel,
        [(block, F32), ((subs, rows, 3 * margin + 2 * functions), BF16)],
        [own, spill_rows, coarse_basis, send, far],
        "local_spread",
        ins=[VMEM] * 3 + [ANY, VMEM],
        limit=8,
    )
    correction, low, image, *sends = call(
        functools.partial(correction_kernel, margin),
        [(block, F32), (block, BF16), ((subs, 4 * margin, width), BF16)] + messages,
        [local, left, margins, local_operator, far_halo, keep, *x_got],
        "correction",
        limit=12,
    )
    got_yo = other(sends[3], "gy")
    got_xo = other(sends[1], "gx")
    got_yp = swap(sends[2], "gy", 1)
    got_xp = swap(sends[0], "gx", 1)

    part, pick, correction = call(
        image_kernel,
        [(block, F32), ((subs, rows, 4 * margin), BF16), (adjoint_rhs.shape, F32)],
        [local_operator, low, adjoint_rhs, correction, spill_rows],
        "image_own",
        out_specs=[VMEM, VMEM, HBM],
        scratch=[dma((subs,))],
        limit=12,
    )
    (residual,) = call(
        functools.partial(residual_kernel, margin),
        [(adjoint_rhs.shape, F32)],
        [part, image, pick, got_xp, got_xo, got_yp, got_yo],
        "residual",
        out_specs=[HBM],
        scratch=[pltpu.VMEM(block, F32), dma((CHUNKS * subs,))],
    )
    return correction, residual


def solution(mesh):
    in_specs = (
        P("gx", "gy", None, None),
        P("gx", "gy", None, None),
        P("gx", "gy", None, None),
        P("gx", "gy", None, None),
        P("gx", "gy", None, None),
        P("gx", "gy", None),
        P(("gx", "gy"), None),
    )
    out_specs = (P("gx", "gy", None, None), P("gx", "gy", None, None))
    return jax.shard_map(body, mesh=mesh, in_specs=in_specs, out_specs=out_specs, check_vma=False)
```

```python
import functools
import jax
import jax.numpy as jnp
from jax import lax
from jax.experimental import pallas as pl
from jax.experimental.pallas import tpu as pltpu
from jax.sharding import PartitionSpec as P

F32 = jnp.float32
BF16 = jnp.bfloat16
CHUNKS = 2
CONTRACT_FIRST = (((0,), (0,)), ((), ()))


def bits_of(count):
    return count.bit_length() - 1


def mask_of(step):
    return (1 << step) - 1


def mirror(bit):
    return (2 << bit) - 2


def swap(value, axis, mask):
    count = lax.axis_size(axis)
    return lax.ppermute(value, axis, [(i, i ^ mask) for i in range(count)])


def other(value, axis):
    count = {name: lax.axis_size(name) for name in ("gx", "gy")}
    pairs = []
    for x in range(count["gx"]):
        for y in range(count["gy"]):
            i = x if axis == "gx" else y
            last = count[axis] - 1
            j = (i - 1 if i % 2 == 0 else i + 1) % count[axis]
            if axis == "gx":
                target = (j, y)
            else:
                target = (x ^ 1, y) if i in (0, last) else (x, j)
            pairs.append((x * count["gy"] + y, target[0] * count["gy"] + target[1]))
    return lax.ppermute(value, ("gx", "gy"), pairs)


def relative_block(block, device, steps):
    left = block ^ device
    place = left * 0
    for step in range(steps):
        place = place | (((left >> step) & 1) << (steps - 1 - step))
    return place


def gathered_place(row, rows, steps):
    per_device = rows >> steps
    left = (row // per_device) ^ lax.axis_index("gy")
    place = row % per_device
    for bit in range(steps):
        place = place + ((left >> bit) & 1) * (rows >> (bit + 1))
    return place


def regathered(value, bit):
    part = value.shape[0] >> (bit + 1)
    pieces = [value[i * part : (i + 1) * part] for i in range(2 << bit)]
    return jnp.concatenate([pieces[i ^ 1] for i in range(2 << bit)], axis=0)


def halves(value):
    high = value.astype(BF16)
    low = (value - high.astype(F32)).astype(BF16)
    return jnp.concatenate([high, low], axis=1)


def joined(value):
    width = value.shape[1] // 2
    return value[:, :width] + value[:, width:]


def mm(left, right):
    return jnp.dot(left, right, preferred_element_type=F32)


def copies_of(pairs, semaphores):
    copies = [
        pltpu.make_async_copy(source, target, semaphores.at[i])
        for i, (source, target) in enumerate(pairs)
    ]
    for copy in copies:
        copy.start()
    return copies


def terms_kernel(
    steps, steps_y, rhs_hbm, basis_hbm, ids_hbm, keep_ref, send_ref, low_ref, rhs_ref, basis_ref, ids_ref, sems
):
    device = lax.axis_index("gx")
    subs, functions, _ = basis_ref.shape
    pairs = [(ids_hbm, ids_ref)]
    for s in range(subs):
        pairs += [(basis_hbm.at[s, 0], basis_ref.at[s]), (rhs_hbm.at[s, 0], rhs_ref.at[s])]
    copies = copies_of(pairs, sems)
    half, width = keep_ref.shape
    order = 2 * half
    block = order >> steps
    copies[0].wait()
    ids = jnp.concatenate([ids_ref[s] for s in range(subs)], axis=1)
    row = lax.broadcasted_iota(jnp.int32, (16, ids.shape[1]), 0)
    coded = jnp.where(row == 0, ids // 256, jnp.where(row == 1, ids % 256, 0))
    send_ref[half:] = coded.astype(F32).astype(BF16)
    place = relative_block(ids // block, device, steps) * block
    place = place + gathered_place(ids % block, block, steps_y)
    rows = lax.broadcasted_iota(jnp.int32, (order, ids.shape[1]), 0)
    pick = (rows == place).astype(BF16)
    terms = []
    for s in range(subs):
        copies[1 + 2 * s].wait()
        copies[2 + 2 * s].wait()
        value = rhs_ref[s]
        high = value.astype(BF16)
        low = (value - high.astype(F32)).astype(BF16)
        low_ref[s] = high
        terms.append(joined(mm(basis_ref[s], jnp.concatenate([high, low], axis=1))))
    terms = jnp.concatenate(terms, axis=0)
    high = terms.astype(BF16)
    low = (terms - high.astype(F32)).astype(BF16)
    total = mm(jnp.concatenate([pick, pick], axis=1), jnp.concatenate([high, low], axis=0))
    keep_ref[...] = total[:half]
    send_ref[:half] = total[half:].astype(BF16)


def exchange_kernel(places, keep_ref, got_ref, *rest):
    holders, (next_ref, send_ref) = (got_ref, *rest[:-2]), rest[-2:]
    rows = keep_ref.shape[0]
    total = keep_ref[...] + got_ref[:rows].astype(F32)
    next_ref[...] = total
    send_ref[:rows] = total.astype(BF16)
    row = lax.broadcasted_iota(jnp.int32, (send_ref.shape[0] - rows, keep_ref.shape[1]), 0)
    packed = jnp.zeros(row.shape, F32)
    for q, (holder, start, _) in enumerate(places):
        code = holders[holder][start : start + 16].astype(F32)
        packed = jnp.where(row == 2 * q, code[0:1], packed)
        packed = jnp.where(row == 2 * q + 1, code[1:2], packed)
    send_ref[rows:] = packed.astype(BF16)


def halve_kernel(known, keep_ref, got_ref, sent_ref, next_ref, send_ref):
    rows = keep_ref.shape[0]
    half = rows // 2
    total = keep_ref[...] + got_ref[:rows].astype(F32)
    next_ref[...] = total[:half]
    send_ref[:half] = total[half:].astype(BF16)
    send_ref[half : half + known] = sent_ref[rows:]
    send_ref[half + known :] = got_ref[rows:]


def join_kernel(near_ref, far_ref, token_ref, out_ref):
    rows = near_ref.shape[0]
    out_ref[:rows] = near_ref[...]
    out_ref[rows:] = far_ref[...]


def sum_kernel(keep_ref, got_ref, *rest):
    halo_refs, next_ref, send_ref = rest[:-2], rest[-2], rest[-1]
    rows = keep_ref.shape[0]
    total = keep_ref[...] + got_ref[:rows].astype(F32)
    next_ref[...] = total
    send_ref[:rows] = total.astype(BF16)
    at = rows
    for ref in halo_refs:
        send_ref[at : at + ref.shape[0]] = ref[...]
        at += ref.shape[0]


def sum_kernel(bit, keep_ref, got_ref, other_ref, next_ref, send_ref, copy_ref):
    rows = keep_ref.shape[0]
    total = keep_ref[...] + regathered(got_ref[:rows].astype(F32), bit)
    next_ref[...] = total
    send_ref[...] = total.astype(BF16)
    copy_ref[...] = other_ref[...]


def outward(width, groups, subs, send_xp, send_xo, send_yp, send_yo):
    even_x = lax.axis_index("gx") % 2 == 0
    even_y = lax.axis_index("gy") % 2 == 0
    west, east = groups(0, 0), groups(subs - 1, 1)
    send_xp[...] = jnp.where(even_x, east, west)
    send_xo[...] = jnp.where(even_x, west, east)
    for s in range(subs):
        south, north = groups(s, 2), groups(s, 3)
        send_yp[s * width : (s + 1) * width] = jnp.where(even_y, north, south)
        send_yo[s * width : (s + 1) * width] = jnp.where(even_y, south, north)


def solve_kernel(width, inverse_ref, rhs_ref, token_ref, own_ref, margin_ref, *sends):
    subs, rows, _ = own_ref.shape
    for s in range(subs):
        value = mm(inverse_ref[s, 0], rhs_ref[s])
        own_ref[s] = value[:rows]
        margin_ref[s] = value[rows:].astype(BF16)

    def groups(sub, number):
        return margin_ref[sub, number * width : (number + 1) * width]

    outward(width, groups, subs, *sends)


def pick_kernel(places, rows_ref, token_ref, *rest):
    id_refs, out_ref = rest[:-1], rest[-1]
    half, order = rows_ref.shape
    width = id_refs[0].shape[1]
    if out_ref.shape[1] > half:
        out_ref[...] = jnp.zeros(out_ref.shape, BF16)
    names = lax.broadcasted_iota(jnp.int32, (order, width), 0)
    rows = rows_ref[...]
    for q, (holder, start, row) in enumerate(places):
        code = id_refs[holder][start : start + 16].astype(F32)[row : row + 2]
        ids = (code[0:1] * 256.0 + code[1:2]).astype(jnp.int32)
        pick = (names == ids).astype(BF16)
        out_ref[q * width : (q + 1) * width, :half] = mm(rows, pick).T.astype(BF16)
    end = len(places) * width
    if out_ref.shape[0] > end:
        carried_ref = id_refs[-1]
        out_ref[end:, : carried_ref.shape[1]] = carried_ref[...]


def coarse_kernel(bit, near_ref, far_ref, keep_ref, halo_ref, got_ref, next_ref, send_ref):
    rows = keep_ref.shape[0]
    total = keep_ref[...] + regathered(got_ref[...].astype(F32), bit)
    low = total.astype(BF16)
    half = next_ref.shape[0]
    count = near_ref.shape[0]
    left = jnp.concatenate([near_ref[...], far_ref[:count, : rows // 2]], axis=1)
    value = mm(left, low)
    next_ref[...] = value[:half]
    send_ref[:half] = value[half:].astype(BF16)
    send_ref[half:] = halo_ref[...]


def halve_halo_kernel(keep_ref, got_ref, halo_ref, next_ref, send_ref):
    rows = keep_ref.shape[0]
    half = rows // 2
    total = keep_ref[...] + got_ref[:rows].astype(F32)
    next_ref[...] = total[:half]
    send_ref[:half] = total[half:].astype(BF16)
    send_ref[half:] = halo_ref[...]


def spread_pick(rows, spill, sides):
    spill = jnp.concatenate([spill[d : d + 1] for d in sides], axis=1)
    iota = lax.broadcasted_iota(jnp.int32, (rows, spill.shape[1]), 0)
    return (iota == spill).astype(BF16)


def west_east(subs, sub, groups, pair, other, even):
    west = groups(sub - 1, 1) if sub > 0 else jnp.where(even, other, pair)
    east = groups(sub + 1, 0) if sub < subs - 1 else jnp.where(even, pair, other)
    return [west, east]


def south_north(sub, width, pair, other, even):
    rows = slice(sub * width, (sub + 1) * width)
    return [jnp.where(even, other[rows], pair[rows]), jnp.where(even, pair[rows], other[rows])]


def other_neighbour(axis):
    device = lax.axis_index(axis)
    even = device % 2 == 0
    other = jnp.where(even, device - 1, device + 1)
    return device, even, other


def from_other(axis, refs, masks, distance):
    device, even, _ = other_neighbour(axis)
    source = jnp.where(even, device - distance, device + distance)
    size, refs = refs
    value = jnp.zeros((size, refs[0].shape[1]), BF16)
    for ref, mask in zip(refs, masks):
        value = jnp.where((device ^ mask) == source, ref[ref.shape[0] - size :], value)
    return even, value


def inner(axis, value):
    device, count = lax.axis_index(axis), lax.axis_size(axis)
    has = jnp.logical_and(device != 0, device != count - 1)
    return jnp.where(has, value, jnp.zeros(value.shape, value.dtype))


def local_kernel(own_ref, spill_ref, basis_ref, token_ref, far_ref, out_ref, left_ref):
    subs, rows, _ = own_ref.shape
    width = spill_ref.shape[3]
    halo = subs * width
    even = lax.axis_index("gy") % 2 == 0
    pair = far_ref[far_ref.shape[0] - halo :, : own_ref.shape[2]]
    for s in range(subs):
        spill = spill_ref[s, 0]
        near = jnp.where(even, spill[3:4], spill[2:3])
        value = pair[s * width : (s + 1) * width]
        out_ref[s] = own_ref[s] + mm(spread_pick(rows, near, (0,)), value)
        left_ref[s, :, : 2 * width] = spread_pick(rows, spill, (0, 1))
        far = jnp.where(even, spill[2:3], spill[3:4])
        basis = basis_ref[s, 0].astype(F32)
        basis = jnp.concatenate([basis, basis], axis=0).T.astype(BF16)
        left_ref[s, :, 2 * width :] = jnp.concatenate([spread_pick(rows, far, (0,)), basis], axis=1)


def correction_kernel(width, local_ref, left_ref, margin_ref, operator_ref, far_ref, keep_ref, *rest):
    x_refs, (out_ref, low_ref, image_ref, *sends) = rest[:-7], rest[-7:]
    subs, rows, columns = local_ref.shape
    functions = keep_ref.shape[0] // subs
    picked = keep_ref[...] + x_refs[-1][: keep_ref.shape[0]].astype(F32)
    masks = [mask_of(step) for step in range(2, len(x_refs) + 1)]
    even, other = from_other("gx", (width, x_refs[1:]), masks, 1)
    pair = x_refs[0][x_refs[0].shape[0] - width :]
    far = inner("gy", far_ref[...])

    def margins(sub, number):
        return margin_ref[sub, number * width : (number + 1) * width]

    for s in range(subs):
        part = picked[s * functions : (s + 1) * functions]
        high = part.astype(BF16)
        low = (part - high.astype(F32)).astype(BF16)
        values = west_east(subs, s, margins, pair, other, even)
        values += [far[s * width : (s + 1) * width], high, low]
        value = local_ref[s] + mm(left_ref[s], jnp.concatenate(values, axis=0))
        out_ref[s] = value
        low = value.astype(BF16)
        low_ref[s] = low
        image_ref[s] = mm(operator_ref[s, 0, rows:], low).astype(BF16)

    def images(sub, number):
        return image_ref[sub, number * width : (number + 1) * width]

    outward(width, images, subs, *sends)


def image_kernel(
    operator_ref, low_ref, rhs_ref, correction_ref, spill_ref, part_ref, pick_ref, out_ref, sems
):
    subs, rows, _ = low_ref.shape
    copies = copies_of([(correction_ref.at[s], out_ref.at[s, 0]) for s in range(subs)], sems)
    for s in range(subs):
        part_ref[s] = rhs_ref[s, 0] - mm(operator_ref[s, 0, :rows], low_ref[s])
        pick_ref[s] = spread_pick(rows, spill_ref[s, 0], range(4))
    for copy in copies:
        copy.wait()


def residual_kernel(
    width, part_ref, image_ref, pick_ref, xp_ref, xo_ref, yp_ref, yo_ref, out_ref, value_ref, sems
):
    subs, rows, _ = part_ref.shape
    even_x = lax.axis_index("gx") % 2 == 0
    even_y = lax.axis_index("gy") % 2 == 0

    def margins(sub, number):
        return image_ref[sub, number * width : (number + 1) * width]

    other_x, other_y = inner("gx", xo_ref[...]), inner("gy", yo_ref[...])
    copies = []
    tile = rows // CHUNKS
    for s in range(subs):
        values = west_east(subs, s, margins, xp_ref[...], other_x, even_x)
        values += south_north(s, width, yp_ref[...], other_y, even_y)
        values = jnp.concatenate(values, axis=0)
        for at in range(0, rows, tile):
            part = slice(at, at + tile)
            value_ref[s, part] = part_ref[s, part] - mm(pick_ref[s, part], values)
            source, target = value_ref.at[s, pl.ds(at, tile)], out_ref.at[s, 0, pl.ds(at, tile)]
            copies.append(pltpu.make_async_copy(source, target, sems.at[len(copies)]))
            copies[-1].start()
    for copy in copies:
        copy.wait()


VMEM = pl.BlockSpec(memory_space=pltpu.VMEM)
HBM = pl.BlockSpec(memory_space=pltpu.HBM)
ANY = pl.BlockSpec(memory_space=pl.ANY)
MIB = 1024 * 1024


def call(kernel, outs, args, name, scratch=(), ins=None, out_specs=None, limit=4, cost=10**9):
    return pl.pallas_call(
        kernel,
        out_shape=[jax.ShapeDtypeStruct(shape, dtype) for shape, dtype in outs],
        in_specs=ins or [VMEM] * len(args),
        out_specs=out_specs or [VMEM] * len(outs),
        scratch_shapes=list(scratch),
        compiler_params=pltpu.CompilerParams(vmem_limit_bytes=limit * MIB),
        cost_estimate=pl.CostEstimate(flops=cost, bytes_accessed=MIB, transcendentals=0),
        name=name,
    )(*args)


def body(
    adjoint_rhs, local_inverse, local_operator, spill_rows, coarse_basis, coarse_ids, coarse_inverse
):
    subs, _, rows, width = adjoint_rhs.shape
    margin = spill_rows.shape[3]
    functions = coarse_ids.shape[2]
    order = coarse_inverse.shape[1]
    count_x, count_y = lax.axis_size("gx"), lax.axis_size("gy")
    steps_x, steps_y = bits_of(count_x), bits_of(count_y)
    listed = subs * functions
    halo = subs * margin
    dma = pltpu.SemaphoreType.DMA
    block = (subs, rows, width)
    messages = [((margin, width), BF16)] * 2 + [((halo, width), BF16)] * 2

    gather_masks = [1 << (steps_y - 1 - i) for i in range(steps_y)]
    near = coarse_inverse
    far = swap(near, "gy", gather_masks[0])

    size = order // 2
    keep, send, low = call(
        functools.partial(terms_kernel, steps_x, steps_y),
        [((size, width), F32), ((size + 16, listed), BF16), (block, BF16)],
        [pltpu.with_memory_space_constraint(x, pltpu.HBM) for x in (adjoint_rhs, coarse_basis, coarse_ids)],
        "coarse_terms",
        ins=[HBM] * 3,
        scratch=[
            pltpu.VMEM(block, F32),
            pltpu.VMEM((subs, functions, rows), BF16),
            pltpu.VMEM(coarse_ids.shape, jnp.int32),
            dma((1 + 2 * subs,)),
        ],
        limit=12,
    )
    got = swap(send, "gx", mask_of(1))
    id_places = [(send, size, 0)]
    for step in range(2, steps_x + 1):
        half = size // 2
        known = 16 * len(id_places)
        id_places = id_places + [(got, size + 16 * i, 0) for i in range(len(id_places))]
        keep, send = call(
            functools.partial(halve_kernel, known),
            [((half, width), F32), ((half + 2 * known, listed), BF16)],
            [keep, got, send],
            "coarse_halve",
        )
        got = swap(send, "gx", 1 << (step - 1))
        size = half
    id_places = id_places + [(got, size + 16 * i, 0) for i in range(len(id_places))]

    holders, places = [got], []
    for q in range(count_x):
        p = 0
        for k in range(1, steps_x + 1):
            p ^= ((q >> (steps_x - k)) & 1) * mask_of(k)
        array, start, _ = id_places[p]
        found = [i for i, holder in enumerate(holders) if holder is array]
        if not found:
            holders.append(array)
            found = [len(holders) - 1]
        places.append((found[0], start, 0))

    own, margins, halo_xp, halo_xo, halo_yp, halo_yo = call(
        functools.partial(solve_kernel, margin),
        [(block, F32), ((subs, 4 * margin, width), BF16)] + messages,
        [local_inverse, low, send],
        "local_solve",
        ins=[VMEM, VMEM, ANY],
        limit=12,
    )

    def join(near, far, token):
        shape = (2 * near.shape[0], near.shape[1])
        return call(
            join_kernel, [(shape, BF16)], [near, far, token], "inverse_join", ins=[VMEM, VMEM, ANY]
        )[0]

    def picked(value, token, places, holders, *carried):
        rows = count_x * listed
        wide = rows + halo * len(carried)
        return call(
            functools.partial(pick_kernel, places),
            [((wide, max(value.shape[0], width * len(carried))), BF16)],
            [value, token, *holders, *carried],
            "inverse_pick",
            ins=[VMEM, ANY] + [VMEM] * (len(holders) + len(carried)),
            limit=8,
        )[0]

    near = join(near, far, own)
    far = swap(near, "gy", gather_masks[1])

    packed = -(-2 * count_x // 16) * 16
    keep, send = call(
        functools.partial(exchange_kernel, places),
        [((size, width), F32), ((size + packed, width), BF16)],
        [keep, got, *holders[1:]],
        "coarse_sum",
    )
    got = swap(send, "gy", mask_of(1))
    for mask in gather_masks[2:-1]:
        near = join(near, far, got)
        far = swap(near, "gy", mask)
    near = join(near, far, got)
    partner = [(0, size + 2 * q // 16 * 16, 2 * q % 16) for q in range(count_x)]
    far = swap(picked(near, got, partner, [got], halo_yp), "gy", gather_masks[-1])
    for bit in range(1, steps_y):
        keep, send, halo_yo = call(
            functools.partial(sum_kernel, bit - 1),
            [((size, width), F32), ((size, width), BF16), ((halo, width), BF16)],
            [keep, got, halo_yo],
            "coarse_sum",
        )
        got = swap(send, "gy", 1 << bit)
    far_halo = other(halo_yo, "gy")

    near = picked(near, send, places, holders)

    half = count_x * listed // 2
    keep, send = call(
        functools.partial(coarse_kernel, steps_y - 1),
        [((half, width), F32), ((half + margin, width), BF16)],
        [near, far, keep, halo_xp, got],
        "coarse_solve",
    )
    x_got = [swap(send, "gx", mask_of(1))]
    for step in range(2, steps_x + 1):
        half = half // 2
        keep, send = call(
            halve_halo_kernel,
            [((half, width), F32), ((half + margin, width), BF16)],
            [keep, x_got[-1], halo_xo],
            "picked_halve",
        )
        x_got.append(swap(send, "gx", mask_of(step)))

    local, left = call(
        local_kernel,
        [(block, F32), ((subs, rows, 3 * margin + 2 * functions), BF16)],
        [own, spill_rows, coarse_basis, send, far],
        "local_spread",
        ins=[VMEM] * 3 + [ANY, VMEM],
        limit=8,
    )
    correction, low, image, *sends = call(
        functools.partial(correction_kernel, margin),
        [(block, F32), (block, BF16), ((subs, 4 * margin, width), BF16)] + messages,
        [local, left, margins, local_operator, far_halo, keep, *x_got],
        "correction",
        limit=12,
    )
    got_yo = other(sends[3], "gy")
    got_xo = other(sends[1], "gx")
    got_yp = swap(sends[2], "gy", 1)
    got_xp = swap(sends[0], "gx", 1)

    part, pick, correction = call(
        image_kernel,
        [(block, F32), ((subs, rows, 4 * margin), BF16), (adjoint_rhs.shape, F32)],
        [local_operator, low, adjoint_rhs, correction, spill_rows],
        "image_own",
        cost=1,
        out_specs=[VMEM, VMEM, HBM],
        scratch=[dma((subs,))],
        limit=12,
    )
    (residual,) = call(
        functools.partial(residual_kernel, margin),
        [(adjoint_rhs.shape, F32)],
        [part, image, pick, got_xp, got_xo, got_yp, got_yo],
        "residual",
        out_specs=[HBM],
        scratch=[pltpu.VMEM(block, F32), dma((CHUNKS * subs,))],
    )
    return correction, residual


def solution(mesh):
    in_specs = (
        P("gx", "gy", None, None),
        P("gx", "gy", None, None),
        P("gx", "gy", None, None),
        P("gx", "gy", None, None),
        P("gx", "gy", None, None),
        P("gx", "gy", None),
        P(("gx", "gy"), None),
    )
    out_specs = (P("gx", "gy", None, None), P("gx", "gy", None, None))
    return jax.shard_map(body, mesh=mesh, in_specs=in_specs, out_specs=out_specs, check_vma=False)
```

```python
import functools
import jax
import jax.numpy as jnp
from jax import lax
from jax.experimental import pallas as pl
from jax.experimental.pallas import tpu as pltpu
from jax.sharding import PartitionSpec as P

F32 = jnp.float32
BF16 = jnp.bfloat16
CHUNKS = 2
CONTRACT_FIRST = (((0,), (0,)), ((), ()))


def bits_of(count):
    return count.bit_length() - 1


def mask_of(step):
    return (1 << step) - 1


def mirror(bit):
    return (2 << bit) - 2


def swap(value, axis, mask):
    count = lax.axis_size(axis)
    return lax.ppermute(value, axis, [(i, i ^ mask) for i in range(count)])


def other(value, axis):
    count = {name: lax.axis_size(name) for name in ("gx", "gy")}
    pairs = []
    for x in range(count["gx"]):
        for y in range(count["gy"]):
            i = x if axis == "gx" else y
            last = count[axis] - 1
            j = (i - 1 if i % 2 == 0 else i + 1) % count[axis]
            if axis == "gx":
                target = (j, y)
            else:
                target = (x ^ 1, y) if i in (0, last) else (x, j)
            pairs.append((x * count["gy"] + y, target[0] * count["gy"] + target[1]))
    return lax.ppermute(value, ("gx", "gy"), pairs)


def relative_block(block, device, steps):
    left = block ^ device
    place = left * 0
    for step in range(steps):
        place = place | (((left >> step) & 1) << (steps - 1 - step))
    return place


def gathered_place(row, rows, steps):
    per_device = rows >> steps
    left = (row // per_device) ^ lax.axis_index("gy")
    place = row % per_device
    for bit in range(steps):
        place = place + ((left >> bit) & 1) * (rows >> (bit + 1))
    return place


def regathered(value, bit):
    part = value.shape[0] >> (bit + 1)
    pieces = [value[i * part : (i + 1) * part] for i in range(2 << bit)]
    return jnp.concatenate([pieces[i ^ 1] for i in range(2 << bit)], axis=0)


def halves(value):
    high = value.astype(BF16)
    low = (value - high.astype(F32)).astype(BF16)
    return jnp.concatenate([high, low], axis=1)


def joined(value):
    width = value.shape[1] // 2
    return value[:, :width] + value[:, width:]


def mm(left, right):
    return jnp.dot(left, right, preferred_element_type=F32)


def copies_of(pairs, semaphores):
    copies = [
        pltpu.make_async_copy(source, target, semaphores.at[i])
        for i, (source, target) in enumerate(pairs)
    ]
    for copy in copies:
        copy.start()
    return copies


def terms_kernel(
    steps, steps_y, rhs_hbm, basis_hbm, ids_hbm, keep_ref, send_ref, low_ref, rhs_ref, basis_ref, ids_ref, sems
):
    device = lax.axis_index("gx")
    subs, functions, _ = basis_ref.shape
    pairs = [(ids_hbm, ids_ref)]
    for s in range(subs):
        pairs += [(basis_hbm.at[s, 0], basis_ref.at[s]), (rhs_hbm.at[s, 0], rhs_ref.at[s])]
    copies = copies_of(pairs, sems)
    half, width = keep_ref.shape
    order = 2 * half
    block = order >> steps
    copies[0].wait()
    ids = jnp.concatenate([ids_ref[s] for s in range(subs)], axis=1)
    row = lax.broadcasted_iota(jnp.int32, (16, ids.shape[1]), 0)
    coded = jnp.where(row == 0, ids // 256, jnp.where(row == 1, ids % 256, 0))
    send_ref[half:] = coded.astype(F32).astype(BF16)
    place = relative_block(ids // block, device, steps) * block
    place = place + gathered_place(ids % block, block, steps_y)
    rows = lax.broadcasted_iota(jnp.int32, (order, ids.shape[1]), 0)
    pick = (rows == place).astype(BF16)
    terms = []
    for s in range(subs):
        copies[1 + 2 * s].wait()
        copies[2 + 2 * s].wait()
        value = rhs_ref[s]
        high = value.astype(BF16)
        low = (value - high.astype(F32)).astype(BF16)
        low_ref[s] = high
        terms.append(joined(mm(basis_ref[s], jnp.concatenate([high, low], axis=1))))
    terms = jnp.concatenate(terms, axis=0)
    high = terms.astype(BF16)
    low = (terms - high.astype(F32)).astype(BF16)
    total = mm(jnp.concatenate([pick, pick], axis=1), jnp.concatenate([high, low], axis=0))
    keep_ref[...] = total[:half]
    send_ref[:half] = total[half:].astype(BF16)


def exchange_kernel(places, keep_ref, got_ref, *rest):
    holders, (next_ref, send_ref) = (got_ref, *rest[:-2]), rest[-2:]
    rows = keep_ref.shape[0]
    total = keep_ref[...] + got_ref[:rows].astype(F32)
    next_ref[...] = total
    send_ref[:rows] = total.astype(BF16)
    row = lax.broadcasted_iota(jnp.int32, (send_ref.shape[0] - rows, keep_ref.shape[1]), 0)
    packed = jnp.zeros(row.shape, F32)
    for q, (holder, start, _) in enumerate(places):
        code = holders[holder][start : start + 16].astype(F32)
        packed = jnp.where(row == 2 * q, code[0:1], packed)
        packed = jnp.where(row == 2 * q + 1, code[1:2], packed)
    send_ref[rows:] = packed.astype(BF16)


def halve_kernel(known, keep_ref, got_ref, sent_ref, next_ref, send_ref):
    rows = keep_ref.shape[0]
    half = rows // 2
    total = keep_ref[...] + got_ref[:rows].astype(F32)
    next_ref[...] = total[:half]
    send_ref[:half] = total[half:].astype(BF16)
    send_ref[half : half + known] = sent_ref[rows:]
    send_ref[half + known :] = got_ref[rows:]


def join_kernel(near_ref, far_ref, token_ref, out_ref):
    rows = near_ref.shape[0]
    out_ref[:rows] = near_ref[...]
    out_ref[rows:] = far_ref[...]


def sum_kernel(keep_ref, got_ref, *rest):
    halo_refs, next_ref, send_ref = rest[:-2], rest[-2], rest[-1]
    rows = keep_ref.shape[0]
    total = keep_ref[...] + got_ref[:rows].astype(F32)
    next_ref[...] = total
    send_ref[:rows] = total.astype(BF16)
    at = rows
    for ref in halo_refs:
        send_ref[at : at + ref.shape[0]] = ref[...]
        at += ref.shape[0]


def sum_kernel(bit, keep_ref, got_ref, other_ref, next_ref, send_ref, copy_ref):
    rows = keep_ref.shape[0]
    total = keep_ref[...] + regathered(got_ref[:rows].astype(F32), bit)
    next_ref[...] = total
    send_ref[...] = total.astype(BF16)
    copy_ref[...] = other_ref[...]


def outward(width, groups, subs, send_xp, send_xo, send_yp, send_yo):
    even_x = lax.axis_index("gx") % 2 == 0
    even_y = lax.axis_index("gy") % 2 == 0
    west, east = groups(0, 0), groups(subs - 1, 1)
    send_xp[...] = jnp.where(even_x, east, west)
    send_xo[...] = jnp.where(even_x, west, east)
    for s in range(subs):
        south, north = groups(s, 2), groups(s, 3)
        send_yp[s * width : (s + 1) * width] = jnp.where(even_y, north, south)
        send_yo[s * width : (s + 1) * width] = jnp.where(even_y, south, north)


def solve_kernel(width, inverse_ref, rhs_ref, token_ref, own_ref, margin_ref, *sends):
    subs, rows, _ = own_ref.shape
    for s in range(subs):
        value = mm(inverse_ref[s, 0], rhs_ref[s])
        own_ref[s] = value[:rows]
        margin_ref[s] = value[rows:].astype(BF16)

    def groups(sub, number):
        return margin_ref[sub, number * width : (number + 1) * width]

    outward(width, groups, subs, *sends)


def pick_kernel(places, rows_ref, token_ref, *rest):
    id_refs, out_ref = rest[:-1], rest[-1]
    half, order = rows_ref.shape
    width = id_refs[0].shape[1]
    if out_ref.shape[1] > half:
        out_ref[...] = jnp.zeros(out_ref.shape, BF16)
    names = lax.broadcasted_iota(jnp.int32, (order, width), 0)
    rows = rows_ref[...]
    for q, (holder, start, row) in enumerate(places):
        code = id_refs[holder][start : start + 16].astype(F32)[row : row + 2]
        ids = (code[0:1] * 256.0 + code[1:2]).astype(jnp.int32)
        pick = (names == ids).astype(BF16)
        out_ref[q * width : (q + 1) * width, :half] = mm(rows, pick).T.astype(BF16)
    end = len(places) * width
    if out_ref.shape[0] > end:
        carried_ref = id_refs[-1]
        out_ref[end:, : carried_ref.shape[1]] = carried_ref[...]


def coarse_kernel(bit, near_ref, far_ref, keep_ref, halo_ref, got_ref, next_ref, send_ref):
    rows = keep_ref.shape[0]
    total = keep_ref[...] + regathered(got_ref[...].astype(F32), bit)
    low = total.astype(BF16)
    half = next_ref.shape[0]
    count = near_ref.shape[0]
    left = jnp.concatenate([near_ref[...], far_ref[:count, : rows // 2]], axis=1)
    value = mm(left, low)
    next_ref[...] = value[:half]
    send_ref[:half] = value[half:].astype(BF16)
    send_ref[half:] = halo_ref[...]


def halve_halo_kernel(keep_ref, got_ref, halo_ref, next_ref, send_ref):
    rows = keep_ref.shape[0]
    half = rows // 2
    total = keep_ref[...] + got_ref[:rows].astype(F32)
    next_ref[...] = total[:half]
    send_ref[:half] = total[half:].astype(BF16)
    send_ref[half:] = halo_ref[...]


def spread_pick(rows, spill, sides):
    spill = jnp.concatenate([spill[d : d + 1] for d in sides], axis=1)
    iota = lax.broadcasted_iota(jnp.int32, (rows, spill.shape[1]), 0)
    return (iota == spill).astype(BF16)


def west_east(subs, sub, groups, pair, other, even):
    west = groups(sub - 1, 1) if sub > 0 else jnp.where(even, other, pair)
    east = groups(sub + 1, 0) if sub < subs - 1 else jnp.where(even, pair, other)
    return [west, east]


def south_north(sub, width, pair, other, even):
    rows = slice(sub * width, (sub + 1) * width)
    return [jnp.where(even, other[rows], pair[rows]), jnp.where(even, pair[rows], other[rows])]


def other_neighbour(axis):
    device = lax.axis_index(axis)
    even = device % 2 == 0
    other = jnp.where(even, device - 1, device + 1)
    return device, even, other


def from_other(axis, refs, masks, distance):
    device, even, _ = other_neighbour(axis)
    source = jnp.where(even, device - distance, device + distance)
    size, refs = refs
    value = jnp.zeros((size, refs[0].shape[1]), BF16)
    for ref, mask in zip(refs, masks):
        value = jnp.where((device ^ mask) == source, ref[ref.shape[0] - size :], value)
    return even, value


def inner(axis, value):
    device, count = lax.axis_index(axis), lax.axis_size(axis)
    has = jnp.logical_and(device != 0, device != count - 1)
    return jnp.where(has, value, jnp.zeros(value.shape, value.dtype))


def local_kernel(own_ref, spill_ref, basis_ref, token_ref, far_ref, out_ref, left_ref):
    subs, rows, _ = own_ref.shape
    width = spill_ref.shape[3]
    halo = subs * width
    even = lax.axis_index("gy") % 2 == 0
    pair = far_ref[far_ref.shape[0] - halo :, : own_ref.shape[2]]
    for s in range(subs):
        spill = spill_ref[s, 0]
        near = jnp.where(even, spill[3:4], spill[2:3])
        value = pair[s * width : (s + 1) * width]
        out_ref[s] = own_ref[s] + mm(spread_pick(rows, near, (0,)), value)
        left_ref[s, :, : 2 * width] = spread_pick(rows, spill, (0, 1))
        far = jnp.where(even, spill[2:3], spill[3:4])
        basis = basis_ref[s, 0].astype(F32)
        basis = jnp.concatenate([basis, basis], axis=0).T.astype(BF16)
        left_ref[s, :, 2 * width :] = jnp.concatenate([spread_pick(rows, far, (0,)), basis], axis=1)


def correction_kernel(width, local_ref, left_ref, margin_ref, operator_ref, far_ref, keep_ref, *rest):
    x_refs, (out_ref, low_ref, image_ref, *sends) = rest[:-7], rest[-7:]
    subs, rows, columns = local_ref.shape
    functions = keep_ref.shape[0] // subs
    picked = keep_ref[...] + x_refs[-1][: keep_ref.shape[0]].astype(F32)
    masks = [mask_of(step) for step in range(2, len(x_refs) + 1)]
    even, other = from_other("gx", (width, x_refs[1:]), masks, 1)
    pair = x_refs[0][x_refs[0].shape[0] - width :]
    far = inner("gy", far_ref[...])

    def margins(sub, number):
        return margin_ref[sub, number * width : (number + 1) * width]

    for s in range(subs):
        part = picked[s * functions : (s + 1) * functions]
        high = part.astype(BF16)
        low = (part - high.astype(F32)).astype(BF16)
        values = west_east(subs, s, margins, pair, other, even)
        values += [far[s * width : (s + 1) * width], high, low]
        value = local_ref[s] + mm(left_ref[s], jnp.concatenate(values, axis=0))
        out_ref[s] = value
        low = value.astype(BF16)
        low_ref[s] = low
        image_ref[s] = mm(operator_ref[s, 0, rows:], low).astype(BF16)

    def images(sub, number):
        return image_ref[sub, number * width : (number + 1) * width]

    outward(width, images, subs, *sends)


def image_kernel(
    operator_ref, low_ref, rhs_ref, correction_ref, spill_ref, part_ref, pick_ref, out_ref, sems
):
    subs, rows, _ = low_ref.shape
    copies = copies_of([(correction_ref.at[s], out_ref.at[s, 0]) for s in range(subs)], sems)
    for s in range(subs):
        part_ref[s] = rhs_ref[s, 0] - mm(operator_ref[s, 0, :rows], low_ref[s])
        pick_ref[s] = spread_pick(rows, spill_ref[s, 0], range(4))
    for copy in copies:
        copy.wait()


def residual_kernel(
    width, part_ref, image_ref, pick_ref, xp_ref, xo_ref, yp_ref, yo_ref, out_ref, value_ref, sems
):
    subs, rows, _ = part_ref.shape
    even_x = lax.axis_index("gx") % 2 == 0
    even_y = lax.axis_index("gy") % 2 == 0

    def margins(sub, number):
        return image_ref[sub, number * width : (number + 1) * width]

    other_x, other_y = inner("gx", xo_ref[...]), inner("gy", yo_ref[...])
    copies = []
    tile = rows // CHUNKS
    for s in range(subs):
        values = west_east(subs, s, margins, xp_ref[...], other_x, even_x)
        values += south_north(s, width, yp_ref[...], other_y, even_y)
        values = jnp.concatenate(values, axis=0)
        for at in range(0, rows, tile):
            part = slice(at, at + tile)
            value_ref[s, part] = part_ref[s, part] - mm(pick_ref[s, part], values)
            source, target = value_ref.at[s, pl.ds(at, tile)], out_ref.at[s, 0, pl.ds(at, tile)]
            copies.append(pltpu.make_async_copy(source, target, sems.at[len(copies)]))
            copies[-1].start()
    for copy in copies:
        copy.wait()


VMEM = pl.BlockSpec(memory_space=pltpu.VMEM)
HBM = pl.BlockSpec(memory_space=pltpu.HBM)
ANY = pl.BlockSpec(memory_space=pl.ANY)
MIB = 1024 * 1024


def call(kernel, outs, args, name, scratch=(), ins=None, out_specs=None, limit=4, cost=10**9):
    return pl.pallas_call(
        kernel,
        out_shape=[jax.ShapeDtypeStruct(shape, dtype) for shape, dtype in outs],
        in_specs=ins or [VMEM] * len(args),
        out_specs=out_specs or [VMEM] * len(outs),
        scratch_shapes=list(scratch),
        compiler_params=pltpu.CompilerParams(vmem_limit_bytes=limit * MIB),
        cost_estimate=pl.CostEstimate(flops=cost, bytes_accessed=MIB, transcendentals=0),
        name=name,
    )(*args)


def body(
    adjoint_rhs, local_inverse, local_operator, spill_rows, coarse_basis, coarse_ids, coarse_inverse
):
    subs, _, rows, width = adjoint_rhs.shape
    margin = spill_rows.shape[3]
    functions = coarse_ids.shape[2]
    order = coarse_inverse.shape[1]
    count_x, count_y = lax.axis_size("gx"), lax.axis_size("gy")
    steps_x, steps_y = bits_of(count_x), bits_of(count_y)
    listed = subs * functions
    halo = subs * margin
    dma = pltpu.SemaphoreType.DMA
    block = (subs, rows, width)
    messages = [((margin, width), BF16)] * 2 + [((halo, width), BF16)] * 2

    gather_masks = [1 << (steps_y - 1 - i) for i in range(steps_y)]
    near = coarse_inverse
    far = swap(near, "gy", gather_masks[0])

    size = order // 2
    keep, send, low = call(
        functools.partial(terms_kernel, steps_x, steps_y),
        [((size, width), F32), ((size + 16, listed), BF16), (block, BF16)],
        [pltpu.with_memory_space_constraint(x, pltpu.HBM) for x in (adjoint_rhs, coarse_basis, coarse_ids)],
        "coarse_terms",
        ins=[HBM] * 3,
        scratch=[
            pltpu.VMEM(block, F32),
            pltpu.VMEM((subs, functions, rows), BF16),
            pltpu.VMEM(coarse_ids.shape, jnp.int32),
            dma((1 + 2 * subs,)),
        ],
        limit=12,
    )
    got = swap(send, "gx", mask_of(1))
    id_places = [(send, size, 0)]
    for step in range(2, steps_x + 1):
        half = size // 2
        known = 16 * len(id_places)
        id_places = id_places + [(got, size + 16 * i, 0) for i in range(len(id_places))]
        keep, send = call(
            functools.partial(halve_kernel, known),
            [((half, width), F32), ((half + 2 * known, listed), BF16)],
            [keep, got, send],
            "coarse_halve",
        )
        got = swap(send, "gx", 1 << (step - 1))
        size = half
    id_places = id_places + [(got, size + 16 * i, 0) for i in range(len(id_places))]

    holders, places = [got], []
    for q in range(count_x):
        p = 0
        for k in range(1, steps_x + 1):
            p ^= ((q >> (steps_x - k)) & 1) * mask_of(k)
        array, start, _ = id_places[p]
        found = [i for i, holder in enumerate(holders) if holder is array]
        if not found:
            holders.append(array)
            found = [len(holders) - 1]
        places.append((found[0], start, 0))

    own, margins, halo_xp, halo_xo, halo_yp, halo_yo = call(
        functools.partial(solve_kernel, margin),
        [(block, F32), ((subs, 4 * margin, width), BF16)] + messages,
        [local_inverse, low, send],
        "local_solve",
        ins=[VMEM, VMEM, ANY],
        limit=12,
    )

    def join(near, far, token):
        shape = (2 * near.shape[0], near.shape[1])
        return call(
            join_kernel, [(shape, BF16)], [near, far, token], "inverse_join", ins=[VMEM, VMEM, ANY]
        )[0]

    def picked(value, token, places, holders, *carried):
        rows = count_x * listed
        wide = rows + halo * len(carried)
        return call(
            functools.partial(pick_kernel, places),
            [((wide, max(value.shape[0], width * len(carried))), BF16)],
            [value, token, *holders, *carried],
            "inverse_pick",
            ins=[VMEM, ANY] + [VMEM] * (len(holders) + len(carried)),
            limit=8,
        )[0]

    near = join(near, far, own)
    far = swap(near, "gy", gather_masks[1])

    packed = -(-2 * count_x // 16) * 16
    keep, send = call(
        functools.partial(exchange_kernel, places),
        [((size, width), F32), ((size + packed, width), BF16)],
        [keep, got, *holders[1:]],
        "coarse_sum",
    )
    got = swap(send, "gy", mask_of(1))
    for mask in gather_masks[2:-1]:
        near = join(near, far, got)
        far = swap(near, "gy", mask)
    near = join(near, far, got)
    partner = [(0, size + 2 * q // 16 * 16, 2 * q % 16) for q in range(count_x)]
    far = swap(picked(near, got, partner, [got], halo_yp), "gy", gather_masks[-1])
    last = 0
    for bit in range(steps_y - 1, 0, -1):
        keep, send, halo_yo = call(
            functools.partial(sum_kernel, last),
            [((size, width), F32), ((size, width), BF16), ((halo, width), BF16)],
            [keep, got, halo_yo],
            "coarse_sum",
        )
        got = swap(send, "gy", 1 << bit)
        last = bit
    far_halo = other(halo_yo, "gy")

    near = picked(near, send, places, holders)

    half = count_x * listed // 2
    keep, send = call(
        functools.partial(coarse_kernel, last),
        [((half, width), F32), ((half + margin, width), BF16)],
        [near, far, keep, halo_xp, got],
        "coarse_solve",
    )
    x_got = [swap(send, "gx", mask_of(1))]
    for step in range(2, steps_x + 1):
        half = half // 2
        keep, send = call(
            halve_halo_kernel,
            [((half, width), F32), ((half + margin, width), BF16)],
            [keep, x_got[-1], halo_xo],
            "picked_halve",
        )
        x_got.append(swap(send, "gx", mask_of(step)))

    local, left = call(
        local_kernel,
        [(block, F32), ((subs, rows, 3 * margin + 2 * functions), BF16)],
        [own, spill_rows, coarse_basis, send, far],
        "local_spread",
        ins=[VMEM] * 3 + [ANY, VMEM],
        limit=8,
    )
    correction, low, image, *sends = call(
        functools.partial(correction_kernel, margin),
        [(block, F32), (block, BF16), ((subs, 4 * margin, width), BF16)] + messages,
        [local, left, margins, local_operator, far_halo, keep, *x_got],
        "correction",
        limit=12,
    )
    got_yo = other(sends[3], "gy")
    got_xo = other(sends[1], "gx")
    got_yp = swap(sends[2], "gy", 1)
    got_xp = swap(sends[0], "gx", 1)

    part, pick, correction = call(
        image_kernel,
        [(block, F32), ((subs, rows, 4 * margin), BF16), (adjoint_rhs.shape, F32)],
        [local_operator, low, adjoint_rhs, correction, spill_rows],
        "image_own",
        cost=1,
        out_specs=[VMEM, VMEM, HBM],
        scratch=[dma((subs,))],
        limit=12,
    )
    (residual,) = call(
        functools.partial(residual_kernel, margin),
        [(adjoint_rhs.shape, F32)],
        [part, image, pick, got_xp, got_xo, got_yp, got_yo],
        "residual",
        out_specs=[HBM],
        scratch=[pltpu.VMEM(block, F32), dma((CHUNKS * subs,))],
    )
    return correction, residual


def solution(mesh):
    in_specs = (
        P("gx", "gy", None, None),
        P("gx", "gy", None, None),
        P("gx", "gy", None, None),
        P("gx", "gy", None, None),
        P("gx", "gy", None, None),
        P("gx", "gy", None),
        P(("gx", "gy"), None),
    )
    out_specs = (P("gx", "gy", None, None), P("gx", "gy", None, None))
    return jax.shard_map(body, mesh=mesh, in_specs=in_specs, out_specs=out_specs, check_vma=False)
```
